256 devices in a mesh: dp: 4 (over y), seq: 64 (over x, z, core).
Axes of the slice: x: 4, y: 4, z: 8, core: 2. Of those that a mesh axis runs over, the one named last changes fastest.
Arguments:
- hidden_in: bfloat16 [65536, 2048], P(('dp', 'seq')), parts along dimension 0, may hold values from -6 to 6
- lin_query: bfloat16 [65536, 1024], P(('dp', 'seq')), parts along dimension 0, may hold values from -6 to 6
- lin_key: bfloat16 [65536, 256], P(('dp', 'seq')), parts along dimension 0, may hold values from -6 to 6
- lin_value: bfloat16 [65536, 256], P(('dp', 'seq')), parts along dimension 0, may hold values from -6 to 6
- lin_gain: float32 [1024], replicated, may hold values from 0.1 to 1.9
- lin_out_weight: bfloat16 [1024, 2048], replicated, may hold values from -0.1875 to 0.1875
- soft_gain: float32 [2048], replicated, may hold values from 0.1 to 1.9
- soft_wq: bfloat16 [2048, 1024], replicated, may hold values from -4 to 4
- soft_wk: bfloat16 [2048, 256], replicated, may hold values from -4 to 4
- soft_wv: bfloat16 [2048, 256], replicated, may hold values from -0.125 to 0.125
- pattern: int32 [2, 128, 18], replicated, may hold values from 0 to 127, as said below
Outputs:
- attended: bfloat16 [65536, 1024], P(('dp', 'seq')), parts along dimension 0
The draws below stay inside these ranges and needn't reach their ends.
There are 4 independent parts, one for each index of `dp`. The reference program is written for one: setup_inputs(seed, part) draws one part's arguments, and reference() takes and returns one part's arrays. A program takes and returns all parts, laid end to end along the dimension named above; an argument that names none is the same for every part. Nothing has to cross between parts.
Inputs may be any that keep to these rules, and one draw needn't show every extreme that they name: pattern[g, b, 0] = b and pattern[g, b, 1] = max(b - 1, 0); every entry of row b lies between 0 and b; for each key-value head and the 2 query blocks held by one device, the entries in slots 2 to 17 of those rows that lie in another device's tokens all name the same key block of that device.
All inputs are finite; a program needn't handle non-finite values.
Results may differ from the reference program's by a relative error of at most 0.035.
Values may be sent and summed in bfloat16 or wider, within the bound.
A program may use at most 128 MiB of HBM per device.

```python
import jax
import jax.numpy as jnp
from jax import lax

D = 2048
HEAD_DIM = 128
HEADS = 8
KV_HEADS = 2
BLOCK = 128
SEL = 18
TOK_DEV = 256
TOKENS = 16384
NBLK = 128
Q_DIM = 1024
KV_DIM = 256


def query_base(key):
    return jax.random.normal(jax.random.fold_in(key, 71), (D, HEADS * HEAD_DIM), jnp.float32) * D ** (-0.5)


def draw_soft_wq(key, part):
    return jnp.clip(query_base(key), -4.0, 4.0).astype(jnp.bfloat16)


def draw_soft_wk(key, part):
    noise = jax.random.normal(jax.random.fold_in(key, 72), (D, KV_HEADS * HEAD_DIM), jnp.float32) * D ** (-0.5)
    return jnp.clip(noise, -4.0, 4.0).astype(jnp.bfloat16)


def draw_pattern(key, part):
    per_dev = TOK_DEV // BLOCK
    dev_count = NBLK // per_dev
    far_count = per_dev * (SEL - 2)
    block_ids = jnp.arange(NBLK, dtype=jnp.int32)
    devices = jnp.arange(dev_count, dtype=jnp.int32)
    noise = jax.random.randint(jax.random.fold_in(key, 81), (KV_HEADS, dev_count, dev_count), 0, 1 << 20)
    before = devices[None, None, :] < devices[None, :, None]
    ranking = jnp.where(before, noise, 1 << 20) * dev_count + devices[None, None, :]
    order = jnp.argsort(ranking, axis=-1, stable=True).astype(jnp.int32)
    limits = jnp.maximum(devices, 1)
    slots = jnp.arange(far_count, dtype=jnp.int32)[None, :] % limits[:, None]
    slots = jnp.broadcast_to(slots[None], (KV_HEADS, dev_count, far_count))
    chosen = jnp.take_along_axis(order, slots, axis=-1)
    offsets = jax.random.randint(jax.random.fold_in(key, 82), (KV_HEADS, dev_count), 0, per_dev)
    far_entries = chosen * per_dev + offsets[:, :, None]
    far_entries = far_entries.reshape(KV_HEADS, NBLK, SEL - 2)
    far_entries = jnp.minimum(far_entries, block_ids[None, :, None])
    first = jnp.broadcast_to(block_ids[None, :, None], (KV_HEADS, NBLK, 1))
    second = jnp.broadcast_to(jnp.maximum(block_ids - 1, 0)[None, :, None], (KV_HEADS, NBLK, 1))
    return jnp.concatenate([first, second, far_entries], axis=2).astype(jnp.int32)


def levels(rng, shape, shards, least, high):
    def one(position, parts):
        draws = jax.random.uniform(jax.random.fold_in(jax.random.fold_in(rng, 6), position), (parts,), jnp.float32, least / len(shards), high / len(shards))
        return jnp.repeat(jnp.exp(draws), shape[position] // parts).reshape((-1,) + (1,) * (len(shape) - position - 1))

    gain = one(*shards[0])
    for cut in shards[1:]:
        gain = gain * one(*cut)
    return gain


def bell_draw(stream_key, extent, deviation, limit, pieces=(), held_as=jnp.bfloat16):
    values = deviation * jax.random.normal(stream_key, extent, jnp.float32)
    if pieces:
        values = values * levels(stream_key, extent, pieces, -0.22, 0.18)
    return jnp.clip(values, -limit, limit).astype(held_as)


def setup_inputs(seed: int = 0, part: int = 0) -> dict:
    splits = jax.random.split(jax.random.key(seed), 12)
    part_keys = jax.random.split(jax.random.fold_in(splits[11], part), 12)
    return {
        "hidden_in": bell_draw(part_keys[0], (TOKENS, D), 1.0, 6.0, ((0, 64),)),
        "lin_query": bell_draw(part_keys[1], (TOKENS, Q_DIM), 1.0, 6.0, ((0, 64),)),
        "lin_key": bell_draw(part_keys[2], (TOKENS, KV_DIM), 1.0, 6.0, ((0, 64),)),
        "lin_value": bell_draw(part_keys[3], (TOKENS, KV_DIM), 1.0, 6.0, ((0, 64),)),
        "lin_gain": jnp.clip(1.0 + 0.18 * jax.random.normal(splits[4], (Q_DIM,), jnp.float32), 0.1, 1.9),
        "lin_out_weight": bell_draw(splits[5], (Q_DIM, D), Q_DIM ** -0.5, 0.1875),
        "soft_gain": jnp.clip(1.0 + 0.18 * jax.random.normal(splits[6], (D,), jnp.float32), 0.1, 1.9),
        "soft_wq": draw_soft_wq(jax.random.fold_in(splits[11], 71), part),
        "soft_wk": draw_soft_wk(jax.random.fold_in(splits[11], 71), part),
        "soft_wv": bell_draw(splits[9], (D, KV_DIM), D ** -0.5, 0.125),
        "pattern": draw_pattern(jax.random.fold_in(splits[11], 71), part),
    }


EPSILON = 1e-06

def linear_mixer(lin_query, lin_key, lin_value):
    blocks_total = lin_query.shape[0] // BLOCK
    per_group = HEADS // KV_HEADS
    queries = lin_query.reshape(blocks_total, BLOCK, KV_HEADS, per_group, HEAD_DIM).astype(jnp.float32)
    keys_all = lin_key.reshape(blocks_total, BLOCK, KV_HEADS, HEAD_DIM).astype(jnp.float32)
    values_all = lin_value.reshape(blocks_total, BLOCK, KV_HEADS, HEAD_DIM).astype(jnp.float32)
    positions = jnp.arange(BLOCK)
    causal = positions[:, None] >= positions[None, :]

    def advance(state, inputs):
        query_block, key_block, value_block = inputs
        inter = jnp.einsum('tgpd,gde->tgpe', query_block, state, precision=lax.Precision.HIGHEST)
        scores = jnp.einsum('tgpd,sgd->gpts', query_block, key_block, precision=lax.Precision.HIGHEST)
        scores = jnp.where(causal, scores, 0.0)
        rounded = lax.optimization_barrier(scores.astype(jnp.bfloat16)).astype(jnp.float32)
        intra = jnp.einsum('gpts,sge->tgpe', rounded, value_block, precision=lax.Precision.HIGHEST)
        updated = state + jnp.einsum('tgd,tge->gde', key_block, value_block, precision=lax.Precision.HIGHEST)
        return (updated, inter + intra)
    start = jnp.zeros((KV_HEADS, HEAD_DIM, HEAD_DIM), jnp.float32)
    final_state, mixed = lax.scan(advance, start, (queries, keys_all, values_all))
    return mixed.reshape(-1, HEADS, HEAD_DIM)

def sparse_attention(soft_query, packed, pattern):
    blocks_total = packed.shape[0] // BLOCK
    per_group = HEADS // KV_HEADS
    listed = pattern.shape[2]
    table = packed.reshape(blocks_total, BLOCK, KV_HEADS, 2 * HEAD_DIM)
    queries = soft_query.reshape(blocks_total, BLOCK, KV_HEADS, per_group, HEAD_DIM)
    group_ids = jnp.arange(KV_HEADS)[:, None]
    rows_here = jnp.arange(BLOCK)
    columns = jnp.arange(listed * BLOCK)
    causal = (columns[None, :] >= BLOCK) | (columns[None, :] <= rows_here[:, None])
    earlier = jnp.arange(listed)[None, :] < jnp.arange(listed)[:, None]
    scale = HEAD_DIM ** (-0.5)

    def one_block(inputs):
        query_block, entries = inputs
        tiles = table[entries, :, group_ids, :]
        tiles = tiles.reshape(KV_HEADS, listed * BLOCK, 2 * HEAD_DIM).astype(jnp.float32)
        keys_tile = tiles[:, :, :HEAD_DIM]
        values_tile = tiles[:, :, HEAD_DIM:]
        same = entries[:, :, None] == entries[:, None, :]
        repeated = jnp.any(same & earlier[None], axis=-1)
        live = jnp.repeat(jnp.logical_not(repeated), BLOCK, axis=-1)
        allowed = live[:, None, None, :] & causal[None, None]
        scores = jnp.einsum('tgpd,gkd->gptk', query_block.astype(jnp.float32), keys_tile, precision=lax.Precision.HIGHEST) * scale
        highest = lax.optimization_barrier(jnp.max(jnp.where(allowed, scores, -jnp.inf), axis=-1, keepdims=True))
        weights = jnp.where(allowed, jnp.exp(scores - highest), 0.0)
        total = lax.optimization_barrier(jnp.sum(weights, axis=-1, keepdims=True))
        probs = lax.optimization_barrier((weights / total).astype(jnp.bfloat16)).astype(jnp.float32)
        result = jnp.einsum('gptk,gke->tgpe', probs, values_tile, precision=lax.Precision.HIGHEST)
        return result.reshape(BLOCK, HEADS * HEAD_DIM).astype(jnp.bfloat16)
    outputs = lax.map(one_block, (queries, jnp.transpose(pattern, (1, 0, 2))))
    return outputs.reshape(-1, HEADS * HEAD_DIM)

def reference(hidden_in, lin_query, lin_key, lin_value, lin_gain, lin_out_weight, soft_gain, soft_wq, soft_wk, soft_wv, pattern):
    mixed = linear_mixer(lin_query, lin_key, lin_value)
    normed = mixed * lax.rsqrt(lax.optimization_barrier(jnp.mean(mixed * mixed, axis=-1, keepdims=True)) + EPSILON) * lin_gain.reshape(HEADS, HEAD_DIM)
    normed = normed.reshape(-1, HEADS * HEAD_DIM).astype(jnp.bfloat16)
    branch = jnp.dot(normed, lin_out_weight, preferred_element_type=jnp.float32)
    residual = (hidden_in.astype(jnp.float32) + branch).astype(jnp.bfloat16)
    widened = lax.optimization_barrier(residual).astype(jnp.float32)
    layer_in = (widened * lax.rsqrt(lax.optimization_barrier(jnp.mean(widened * widened, axis=-1, keepdims=True)) + EPSILON) * soft_gain).astype(jnp.bfloat16)
    soft_query = jnp.dot(layer_in, soft_wq, preferred_element_type=jnp.float32).astype(jnp.bfloat16)
    soft_key = jnp.dot(layer_in, soft_wk, preferred_element_type=jnp.float32).astype(jnp.bfloat16)
    soft_value = jnp.dot(layer_in, soft_wv, preferred_element_type=jnp.float32).astype(jnp.bfloat16)
    packed = jnp.concatenate([soft_key.reshape(-1, KV_HEADS, HEAD_DIM), soft_value.reshape(-1, KV_HEADS, HEAD_DIM)], axis=-1)
    return sparse_attention(soft_query, packed, pattern)
```

```python
import math

import jax
import jax.numpy as jnp
from jax import lax
from jax.experimental import pallas as pl
from jax.experimental.pallas import tpu as pltpu
from jax.sharding import PartitionSpec as P

HEAD_DIM = 128
HEADS = 8
KV_HEADS = 2
PER_GROUP = HEADS // KV_HEADS
BLOCK = 128
SEL = 18
TOK = 256
D = 2048
NX, NZ = 4, 8
CHIP_TOK = 2 * TOK
PAIRS = SEL // 2
EPSILON = 1e-06
NEG = -1e30
COEF = HEAD_DIM ** (-0.5) * math.log2(math.e)
F32, BF16 = jnp.float32, jnp.bfloat16
MESH = pl.DeviceIdType.MESH

ROWS_A = 208
ROWS_B = CHIP_TOK - ROWS_A
ORDER = [(0, 0), (0, 1), (1, 1), (0, 2), (1, 2), (0, 3), (1, 3), (0, 4)]


def dot(a, b):
    return jnp.dot(a, b, preferred_element_type=F32)


def dot_nt(a, b):
    return lax.dot_general(a, b, (((1,), (1,)), ((), ())), preferred_element_type=F32)


def dot_tn(a, b):
    return lax.dot_general(a, b, (((0,), (0,)), ((), ())), preferred_element_type=F32)


def kernel(
    pattern, lin_gain, soft_gain, hidden_hbm, lq_hbm, lk_hbm, lv_hbm, wo_hbm, wq_hbm, wk_hbm, wv_hbm,
    o_ref,
    hidden, lq, lk, lv, wo, wq, wkv, st_send, st_recv, tot_send, tot_recv, pre_send, pre_recv,
    block0, lin_scores, normed, resid, layer_in, kv_send, q_send, q_all, table, scores, bias, o_send, o_all,
    load_sem, st_ssem, st_rsem, tot_ssem, tot_rsem, pre_ssem, pre_rsem, sib_ssem, sib_rsem,
    a1_ssem, a1_rsem, a2_ssem, a2_rsem, b1_ssem, b1_rsem, b2_ssem, b2_rsem,
):
    me = lax.axis_index("seq")
    core = lax.rem(me, 2)
    chip = me // 2
    z = lax.rem(chip, NZ)
    x = chip // NZ
    sign = 1 - 2 * core
    row_pos = z * 2 + core

    def dev(cx, cz, cc):
        return {"seq": (lax.rem(cx + 2 * NX, NX) * NZ + lax.rem(cz + 2 * NZ, NZ)) * 2 + cc}

    sibling = dev(x, z, 1 - core)

    def remote(src, dst, ssem, rsem, device):
        return pltpu.make_async_remote_copy(
            src_ref=src, dst_ref=dst, send_sem=ssem, recv_sem=rsem, device_id=device, device_id_type=MESH
        )

    barrier = pltpu.get_barrier_semaphore()
    for i in range(1, 2 * NZ):
        pos = lax.rem(row_pos + i, 2 * NZ)
        pl.semaphore_signal(barrier, inc=1, device_id={"seq": x * 2 * NZ + pos}, device_id_type=MESH)
    for i in range(1, NX):
        pl.semaphore_signal(barrier, inc=1, device_id=dev(x + i, z, core), device_id_type=MESH)

    own_q = pl.ds(pl.multiple_of(core * 512, 512), 512)
    sib_q = pl.ds(pl.multiple_of((1 - core) * 512, 512), 512)
    own_h = pl.ds(pl.multiple_of(core * 128, 128), 128)
    sib_h = pl.ds(pl.multiple_of((1 - core) * 128, 128), 128)
    loads = [
        (lk_hbm, lk),
        (lv_hbm, lv),
        (lq_hbm, lq),
        (wo_hbm, wo),
        (hidden_hbm, hidden),
        (wk_hbm.at[:, own_h], wkv.at[0, :, 0:128]),
        (wv_hbm.at[:, own_h], wkv.at[0, :, 128:256]),
        (wk_hbm.at[:, sib_h], wkv.at[1, :, 0:128]),
        (wv_hbm.at[:, sib_h], wkv.at[1, :, 128:256]),
        (wq_hbm.at[:, own_q], wq.at[0]),
        (wq_hbm.at[:, sib_q], wq.at[1]),
    ]
    loads = [pltpu.make_async_copy(src, dst, load_sem.at[i]) for i, (src, dst) in enumerate(loads)]
    for copy in loads:
        copy.start()
    loads[0].wait()
    loads[1].wait()

    for g in range(KV_HEADS):
        cols = slice(g * 128, g * 128 + 128)
        first = dot_tn(lk[0:128, cols], lv[0:128, cols])
        second = dot_tn(lk[128:256, cols], lv[128:256, cols])
        block0[g] = first
        st_send[g] = (first + second).reshape(NZ, 16, 128)

    pl.semaphore_wait(barrier, 2 * NZ - 1 + NX - 1)

    st_copies = []
    for i in range(1, 2 * NZ):
        pos = lax.rem(row_pos + i, 2 * NZ)
        copy = remote(
            st_send.at[lax.rem(pos, 2), pos // 2], st_recv.at[row_pos], st_ssem.at[i - 1], st_rsem.at[i - 1],
            {"seq": x * 2 * NZ + pos},
        )
        copy.start()
        st_copies.append(copy)
    st_recv[row_pos] = st_send[core, z]

    loads[2].wait()
    tri = lax.broadcasted_iota(jnp.int32, (128, 128), 0) >= lax.broadcasted_iota(jnp.int32, (128, 128), 1)
    tri4 = jnp.concatenate([tri] * PER_GROUP, axis=0)

    def stacked(n, g):
        return jnp.concatenate(
            [lq[n * 128 : n * 128 + 128, (g * PER_GROUP + h) * 128 : (g * PER_GROUP + h) * 128 + 128] for h in range(PER_GROUP)],
            axis=0,
        )

    for n in range(2):
        for g in range(KV_HEADS):
            keys = lk[n * 128 : n * 128 + 128, g * 128 : g * 128 + 128]
            lin_scores[n, g] = jnp.where(tri4, dot_nt(stacked(n, g), keys), 0.0).astype(BF16)

    for copy in st_copies:
        copy.wait()
    total = st_recv[0]
    for i in range(1, 2 * NZ):
        total = total + st_recv[i]
    tot_send[...] = total
    tot_copies = []
    for i in range(1, NX):
        copy = remote(tot_send, tot_recv.at[i - 1], tot_ssem.at[i - 1], tot_rsem.at[i - 1], dev(x + i, z, core))
        copy.start()
        tot_copies.append(copy)
    for copy in tot_copies:
        copy.wait()
    running = jnp.zeros((16, 128), F32)
    for i in range(1, NX):
        running = running + jnp.where(x - i >= 0, tot_recv[i - 1], 0.0)
    for i in range(2 * NZ):
        pre_send[i] = running
        running = running + st_recv[i]
    pre_copies = []
    for i in range(1, 2 * NZ):
        pos = lax.rem(row_pos + i, 2 * NZ)
        copy = remote(
            pre_send.at[pos], pre_recv.at[core, z], pre_ssem.at[i - 1], pre_rsem.at[i - 1], {"seq": x * 2 * NZ + pos}
        )
        copy.start()
        pre_copies.append(copy)
    pre_recv[core, z] = pre_send[row_pos]
    for copy in pre_copies:
        copy.wait()

    for n in range(2):
        for g in range(KV_HEADS):
            state = pre_recv[g].reshape(128, 128)
            if n == 1:
                state = state + block0[g]
            high = state.astype(BF16)
            low = (state - high.astype(F32)).astype(BF16)
            qs = stacked(n, g)
            mix = dot(
                jnp.concatenate([qs, qs, lin_scores[n, g]], axis=1),
                jnp.concatenate([high, low, lv[n * 128 : n * 128 + 128, g * 128 : g * 128 + 128]], axis=0),
            )
            mix = mix * lax.rsqrt(jnp.mean(mix * mix, axis=-1, keepdims=True) + EPSILON)
            for h in range(PER_GROUP):
                cols = slice((g * PER_GROUP + h) * 128, (g * PER_GROUP + h) * 128 + 128)
                normed[n * 128 : n * 128 + 128, cols] = (mix[h * 128 : h * 128 + 128] * lin_gain[:, cols]).astype(BF16)

    loads[3].wait()
    loads[4].wait()
    squares = jnp.zeros((TOK, 128), F32)
    for t in range(4):
        cols = slice(t * 512, t * 512 + 512)
        res = (hidden[:, cols].astype(F32) + dot(normed[...], wo[:, cols])).astype(BF16)
        resid[:, cols] = res
        wide = res.astype(F32)
        wide = wide * wide
        for s in range(4):
            squares = squares + wide[:, s * 128 : s * 128 + 128]
    factor = lax.rsqrt(jnp.sum(squares, axis=-1, keepdims=True) * (1.0 / D) + EPSILON)
    for t in range(4):
        cols = slice(t * 512, t * 512 + 512)
        layer_in[:, cols] = (resid[:, cols].astype(F32) * factor * soft_gain[:, cols]).astype(BF16)

    for i in range(5, 9):
        loads[i].wait()
    flat = table.reshape(NX * NZ * CHIP_TOK, 256)
    my_rows = pl.ds(pl.multiple_of(me * TOK, TOK), TOK)
    kv_send[...] = dot(layer_in[...], wkv[1]).astype(BF16)
    kv_copy = remote(kv_send, flat.at[my_rows], sib_ssem.at[0], sib_rsem.at[0], sibling)
    kv_copy.start()
    flat[my_rows] = dot(layer_in[...], wkv[0]).astype(BF16)
    kv_copy.wait()

    rows_a, rows_b = (0, ROWS_A), (ROWS_A, ROWS_B)
    pending = []

    def send(src_chip, rows, ssem, rsem, device):
        part = flat.at[pl.ds(pl.multiple_of(src_chip * CHIP_TOK + rows[0], 16), rows[1])]
        copy = remote(part, part, ssem, rsem, device)
        copy.start()
        pending.append(copy)
        return copy

    def row_chip(direction, distance):
        step = -sign if direction == 0 else sign
        return x * NZ + lax.rem(z + step * distance + NZ, NZ)

    def col_chip(cx, cz):
        return lax.rem(cx + NX, NX) * NZ + lax.rem(cz + NZ, NZ)

    def z_dev(direction):
        return dev(x, z + (sign if direction == 0 else -sign), core)

    a1 = [send(chip, rows_a, a1_ssem.at[i - 1], a1_rsem.at[i - 1], dev(x + i, z, core)) for i in (1, 3, 2)]
    b1 = {}
    b2 = {}

    def send_b1(direction, t):
        b1[direction, t] = send(
            row_chip(direction, t - 1), rows_b, b1_ssem.at[direction, t - 1], b1_rsem.at[direction, t - 1], z_dev(direction)
        )

    def send_b2(r):
        src = row_chip(*ORDER[r])
        for j, dx in enumerate((1, -1)):
            b2[r, j] = send(src, rows_b, b2_ssem.at[r, j], b2_rsem.at[r, j], dev(x + dx, z, core))

    def forward_b2(r):
        j = r % 2
        b2[r, j].wait_recv()
        direction, distance = ORDER[r]
        step = -sign if direction == 0 else sign
        src = col_chip(x + (-1 if j == 0 else 1), z + step * distance)
        b2[r, 2] = send(src, rows_b, b2_ssem.at[r, 2], b2_rsem.at[r, 2], dev(x + (1 if j == 0 else -1), z, core))

    a2 = {}

    def send_a2(direction, t):
        step = -sign if direction == 0 else sign
        for i in range(NX):
            src = col_chip(x + i, z + step * (t - 1))
            a2[direction, t, i] = send(
                src, rows_a, a2_ssem.at[direction, t - 1, i], a2_rsem.at[direction, t - 1, i], z_dev(direction)
            )

    send_b1(0, 1)
    send_b1(1, 1)
    send_b2(0)

    loads[9].wait()
    loads[10].wait()

    def put_queries(part, write):
        q = dot(layer_in[...], wq[part]).astype(BF16)
        for n in range(2):
            for h in range(PER_GROUP):
                write(n, h, q[n * 128 : n * 128 + 128, h * 128 : h * 128 + 128])

    def write_send(n, h, value):
        q_send[n, h * 128 : h * 128 + 128, :] = value

    def write_own(n, h, value):
        q_all[core * 2 + n, h * 128 : h * 128 + 128, :] = value

    put_queries(1, write_send)
    q_copy = remote(q_send, q_all.at[pl.ds(core * 2, 2)], sib_ssem.at[1], sib_rsem.at[1], sibling)
    q_copy.start()

    for copy in a1:
        copy.wait_recv()
    send_a2(0, 1)
    send_a2(1, 1)
    put_queries(0, write_own)

    def find_repeats(i, carry):
        entries = [pattern[core, chip * 4 + i, j] for j in range(SEL)]
        for j in range(SEL):
            value = jnp.float32(0.0)
            for e in range(j):
                value = jnp.where(entries[e] == entries[j], jnp.float32(NEG), value)
            bias[i, j] = value
        return carry

    lax.fori_loop(0, 4, find_repeats, 0)

    b1[0, 1].wait_recv()
    send_b1(0, 2)
    send_b2(1)
    b1[1, 1].wait_recv()
    send_b1(1, 2)
    send_b2(2)
    forward_b2(0)
    b1[0, 2].wait_recv()
    send_b1(0, 3)
    send_b2(3)
    b1[1, 2].wait_recv()
    send_b1(1, 3)
    send_b2(4)
    forward_b2(1)
    b1[0, 3].wait_recv()
    send_b1(0, 4)
    send_b2(5)
    b1[1, 3].wait_recv()
    send_b2(6)
    forward_b2(2)
    b1[0, 4].wait_recv()
    send_b2(7)
    for i in range(NX):
        a2[0, 1, i].wait_recv()
    send_a2(0, 2)
    for i in range(NX):
        a2[1, 1, i].wait_recv()
    send_a2(1, 2)
    forward_b2(3)
    forward_b2(4)
    for i in range(NX):
        a2[0, 2, i].wait_recv()
    send_a2(0, 3)
    for i in range(NX):
        a2[1, 2, i].wait_recv()
    send_a2(1, 3)
    forward_b2(5)
    forward_b2(6)
    for i in range(NX):
        a2[0, 3, i].wait_recv()
    send_a2(0, 4)
    forward_b2(7)
    for i in range(NX):
        a2[1, 3, i].wait_recv()
        a2[0, 4, i].wait_recv()
    for r in range(NZ):
        b2[r, 1 - r % 2].wait_recv()
        b2[r, 2].wait_recv()
    q_copy.wait()
    for copy in pending:
        copy.wait_send()

    def block_of(i, j):
        return pattern[core, chip * 4 + i, j]

    def attend(part, n):
        i = (1 - core if part == 0 else core) * 2 + n
        q = q_all[i]
        top = jnp.full((512, 128), NEG, F32)
        for p in range(PAIRS):
            keys = jnp.concatenate([table[block_of(i, 2 * p)][:, 0:128], table[block_of(i, 2 * p + 1)][:, 0:128]], axis=0)
            s = dot_nt(q, keys) * COEF
            left, right = s[:, 0:128] + bias[i, 2 * p], s[:, 128:256] + bias[i, 2 * p + 1]
            if p == 0:
                left = jnp.where(tri4, left, NEG)
            scores[p, :, 0:128] = left
            scores[p, :, 128:256] = right
            top = jnp.maximum(top, jnp.maximum(left, right))
        top = jnp.max(top, axis=-1, keepdims=True)
        total = jnp.zeros((512, 128), F32)
        out = jnp.zeros((512, 128), F32)
        for p in range(PAIRS):
            values = jnp.concatenate([table[block_of(i, 2 * p)][:, 128:256], table[block_of(i, 2 * p + 1)][:, 128:256]], axis=0)
            w = jnp.exp2(scores[p] - top)
            total = total + (w[:, 0:128] + w[:, 128:256])
            out = out + dot(w.astype(BF16), values)
        out = (out / jnp.sum(total, axis=-1, keepdims=True)).astype(BF16)
        rows = pl.ds(pl.multiple_of(n * 128, 128), 128)
        for h in range(PER_GROUP):
            if part == 0:
                o_send[rows, h * 128 : h * 128 + 128] = out[h * 128 : h * 128 + 128]
            else:
                o_all[core, rows, h * 128 : h * 128 + 128] = out[h * 128 : h * 128 + 128]

    @pl.loop(0, 2)
    def _(n):
        attend(0, n)

    o_copy = remote(o_send, o_all.at[core], sib_ssem.at[2], sib_rsem.at[2], sibling)
    o_copy.start()

    @pl.loop(0, 2)
    def _(n):
        attend(1, n)

    o_copy.wait()
    o_ref[:, 0:512] = o_all[0]
    o_ref[:, 512:1024] = o_all[1]


def local(hidden_in, lin_query, lin_key, lin_value, lin_gain, lin_out_weight, soft_gain, soft_wq, soft_wk, soft_wv, pattern):
    dma = pltpu.SemaphoreType.DMA
    vmem, anywhere = pl.BlockSpec(memory_space=pltpu.VMEM), pl.BlockSpec(memory_space=pl.ANY)
    scratch = [
        pltpu.VMEM((TOK, D), BF16),
        pltpu.VMEM((TOK, 1024), BF16),
        pltpu.VMEM((TOK, 256), BF16),
        pltpu.VMEM((TOK, 256), BF16),
        pltpu.VMEM((1024, D), BF16),
        pltpu.VMEM((2, D, 512), BF16),
        pltpu.VMEM((2, D, 256), BF16),
        pltpu.VMEM((2, NZ, 16, 128), F32),
        pltpu.VMEM((2 * NZ, 16, 128), F32),
        pltpu.VMEM((16, 128), F32),
        pltpu.VMEM((NX - 1, 16, 128), F32),
        pltpu.VMEM((2 * NZ, 16, 128), F32),
        pltpu.VMEM((2, NZ, 16, 128), F32),
        pltpu.VMEM((2, 128, 128), F32),
        pltpu.VMEM((2, 2, 512, 128), BF16),
        pltpu.VMEM((TOK, 1024), BF16),
        pltpu.VMEM((TOK, D), BF16),
        pltpu.VMEM((TOK, D), BF16),
        pltpu.VMEM((TOK, 256), BF16),
        pltpu.VMEM((2, 512, 128), BF16),
        pltpu.VMEM((4, 512, 128), BF16),
        pltpu.VMEM((NX * NZ * CHIP_TOK // BLOCK, BLOCK, 256), BF16),
        pltpu.VMEM((PAIRS, 512, 256), F32),
        pltpu.SMEM((4, SEL), F32),
        pltpu.VMEM((TOK, 512), BF16),
        pltpu.VMEM((2, TOK, 512), BF16),
        dma((11,)),
        dma((2 * NZ - 1,)), dma((2 * NZ - 1,)),
        dma((NX - 1,)), dma((NX - 1,)),
        dma((2 * NZ - 1,)), dma((2 * NZ - 1,)),
        dma((3,)), dma((3,)),
        dma((3,)), dma((3,)),
        dma((2, 4, NX)), dma((2, 4, NX)),
        dma((2, 4)), dma((2, 4)),
        dma((NZ, 3)), dma((NZ, 3)),
    ]
    return pl.pallas_call(
        kernel,
        name="mixer_and_attention",
        out_shape=jax.ShapeDtypeStruct((TOK, 1024), BF16),
        in_specs=[pl.BlockSpec(memory_space=pltpu.SMEM), vmem, vmem] + [anywhere] * 8,
        out_specs=vmem,
        scratch_shapes=scratch,
        compiler_params=pltpu.CompilerParams(collective_id=0, has_side_effects=True, vmem_limit_bytes=56 << 20),
    )(
        pattern, lin_gain.reshape(1, 1024), soft_gain.reshape(1, D),
        hidden_in, lin_query, lin_key, lin_value, lin_out_weight, soft_wq, soft_wk, soft_wv,
    )


def solution(mesh):
    whole, split = P(), P(("dp", "seq"), None)
    in_specs = (split, split, split, split) + (whole,) * 7
    return jax.shard_map(local, mesh=mesh, in_specs=in_specs, out_specs=split, check_vma=False)
```

```python
import heapq
import math

import jax
import jax.numpy as jnp
from jax import lax
from jax.experimental import pallas as pl
from jax.experimental.pallas import tpu as pltpu
from jax.sharding import PartitionSpec as P

HEAD_DIM = 128
HEADS = 8
KV_HEADS = 2
PER_GROUP = HEADS // KV_HEADS
BLOCK = 128
SEL = 18
TOK = 256
D = 2048
NX, NZ = 4, 8
CHIP_TOK = 2 * TOK
PAIRS = SEL // 2
EPSILON = 1e-06
NEG = -1e30
COEF = HEAD_DIM ** (-0.5) * math.log2(math.e)
F32, BF16 = jnp.float32, jnp.bfloat16
MESH = pl.DeviceIdType.MESH

ROWS_A = 208
ROWS_B = CHIP_TOK - ROWS_A
ORDER = [(0, 0), (0, 1), (1, 1), (0, 2), (1, 2), (0, 3), (1, 3), (0, 4)]
STEPS = (4, 3)


def plan():
    ready, free, events, arrived, order = {"x": [], "z": []}, {"x": 0.0, "z": 0.0}, [], {}, []

    def add(copy, needs):
        kind, tensor = copy[:2]
        rank = (tensor, ("a1", "b1", "b2", "a2").index(kind), copy[3:] + copy[2:3] if kind in ("b1", "a2") else copy[2:])
        heapq.heappush(ready["x" if kind in ("a1", "b2") else "z"], (rank, copy, needs))

    def react(copy):
        kind, tensor, rest = copy[0], copy[1], copy[2:]
        if kind == "a1":
            add(("a2", tensor, 0, 1, rest[0]), copy)
            add(("a2", tensor, 1, 1, rest[0]), copy)
        elif kind == "b1":
            direction, step = rest
            if step < STEPS[direction]:
                add(("b1", tensor, direction, step + 1), copy)
            add(("b2", tensor, ORDER.index(rest), 0), copy)
            add(("b2", tensor, ORDER.index(rest), 1), copy)
        elif kind == "b2":
            if rest[1] == rest[0] % 2:
                add(("b2", tensor, rest[0], 2), copy)
        elif rest[1] < STEPS[rest[0]]:
            add(("a2", tensor, rest[0], rest[1] + 1, rest[2]), copy)

    for tensor in range(2):
        for i in (1, 3, 2):
            add(("a1", tensor, i), None)
        for i in range(2):
            add(("b1", tensor, i, 1), None)
            add(("b2", tensor, 0, i), None)
            add(("a2", tensor, i, 1, 0), None)
    now, count = 0.0, 0
    while True:
        for link in "xz":
            if free[link] <= now and ready[link]:
                _, copy, needs = heapq.heappop(ready[link])
                order.append((now, copy, needs, True))
                rows = (ROWS_A if copy[0] in ("a1", "a2") else ROWS_B) * (2 if copy[0] == "a1" and copy[2] == 2 else 1)
                free[link] = now + rows * 256 / 95e3
                arrived[copy] = free[link] + 4.0
                order.append((arrived[copy], copy, copy, False))
                for event in ((arrived[copy], count, copy), (free[link], count + 1, None)):
                    heapq.heappush(events, event)
                count += 2
        if not events:
            return [step[1:] for step in sorted(order, key=lambda step: step[0])]
        now, _, copy = heapq.heappop(events)
        if copy:
            react(copy)


def dot(a, b):
    return jnp.dot(a, b, preferred_element_type=F32)


def dot_nt(a, b):
    return lax.dot_general(a, b, (((1,), (1,)), ((), ())), preferred_element_type=F32)


def dot_tn(a, b):
    return lax.dot_general(a, b, (((0,), (0,)), ((), ())), preferred_element_type=F32)


def kernel(
    pattern_t, lin_gain, soft_gain, hidden_hbm, lq_hbm, lk_hbm, lv_hbm, wo_hbm, wq_hbm, wk_hbm, wv_hbm,
    o_ref,
    hidden, lq, lk, lv, wo, wq, wkv, st_send, st_recv, tot_send, tot_recv, pre_send, pre_recv,
    block0, lin_scores, normed, resid, layer_in, kv_send, q_send, q_all, key_table, value_table, scores, probs, top, norms, bias,
    o_send, o_all,
    load_sem, st_ssem, st_rsem, tot_ssem, tot_rsem, pre_ssem, pre_rsem, sib_ssem, sib_rsem,
    a1_ssem, a1_rsem, a2_ssem, a2_rsem, b1_ssem, b1_rsem, b2_ssem, b2_rsem,
):
    me = lax.axis_index("seq")
    core = lax.rem(me, 2)
    chip = me // 2
    z = lax.rem(chip, NZ)
    x = chip // NZ
    sign = 1 - 2 * core
    row_pos = z * 2 + core

    def dev(cx, cz, cc):
        return {"seq": (lax.rem(cx + 2 * NX, NX) * NZ + lax.rem(cz + 2 * NZ, NZ)) * 2 + cc}

    sibling = dev(x, z, 1 - core)

    def remote(src, dst, ssem, rsem, device):
        return pltpu.make_async_remote_copy(
            src_ref=src, dst_ref=dst, send_sem=ssem, recv_sem=rsem, device_id=device, device_id_type=MESH
        )

    barrier = pltpu.get_barrier_semaphore()
    for i in range(1, 2 * NZ):
        pos = lax.rem(row_pos + i, 2 * NZ)
        pl.semaphore_signal(barrier, inc=1, device_id={"seq": x * 2 * NZ + pos}, device_id_type=MESH)
    for i in range(1, NX):
        pl.semaphore_signal(barrier, inc=1, device_id=dev(x + i, z, core), device_id_type=MESH)

    own_q = pl.ds(pl.multiple_of(core * 512, 512), 512)
    sib_q = pl.ds(pl.multiple_of((1 - core) * 512, 512), 512)
    own_h = pl.ds(pl.multiple_of(core * 128, 128), 128)
    sib_h = pl.ds(pl.multiple_of((1 - core) * 128, 128), 128)
    loads = [
        (lk_hbm, lk),
        (lv_hbm, lv),
        (lq_hbm, lq),
        (wo_hbm, wo),
        (hidden_hbm, hidden),
        (wk_hbm.at[:, own_h], wkv.at[0, :, 0:128]),
        (wv_hbm.at[:, own_h], wkv.at[0, :, 128:256]),
        (wk_hbm.at[:, sib_h], wkv.at[1, :, 0:128]),
        (wv_hbm.at[:, sib_h], wkv.at[1, :, 128:256]),
        (wq_hbm.at[:, own_q], wq.at[0]),
        (wq_hbm.at[:, sib_q], wq.at[1]),
    ]
    loads = [pltpu.make_async_copy(src, dst, load_sem.at[i]) for i, (src, dst) in enumerate(loads)]
    for copy in loads[:3]:
        copy.start()
    loads[0].wait()
    loads[1].wait()

    for g in range(KV_HEADS):
        cols = slice(g * 128, g * 128 + 128)
        first = dot_tn(lk[0:128, cols], lv[0:128, cols])
        second = dot_tn(lk[128:256, cols], lv[128:256, cols])
        block0[g] = first.astype(BF16)
        st_send[g] = (first + second).astype(BF16).reshape(NZ, 16, 128)

    pl.semaphore_wait(barrier, 2 * NZ - 1 + NX - 1)

    st_copies = []
    for i in range(1, 2 * NZ):
        pos = lax.rem(row_pos + i, 2 * NZ)
        copy = remote(
            st_send.at[lax.rem(pos, 2), pos // 2], st_recv.at[row_pos], st_ssem.at[i - 1], st_rsem.at[i - 1],
            {"seq": x * 2 * NZ + pos},
        )
        copy.start()
        st_copies.append(copy)
    for copy in loads[3:]:
        copy.start()
    st_recv[row_pos] = st_send[core, z]

    loads[2].wait()
    tri = lax.broadcasted_iota(jnp.int32, (128, 128), 0) >= lax.broadcasted_iota(jnp.int32, (128, 128), 1)
    tri4 = jnp.concatenate([tri] * PER_GROUP, axis=0)

    def stacked(n, g):
        return jnp.concatenate(
            [lq[n * 128 : n * 128 + 128, (g * PER_GROUP + h) * 128 : (g * PER_GROUP + h) * 128 + 128] for h in range(PER_GROUP)],
            axis=0,
        )

    for n in range(2):
        for g in range(KV_HEADS):
            keys = lk[n * 128 : n * 128 + 128, g * 128 : g * 128 + 128]
            lin_scores[n, g] = jnp.where(tri4, dot_nt(stacked(n, g), keys), 0.0).astype(BF16)

    for copy in st_copies:
        copy.wait()
    total = st_recv[0].astype(F32)
    for i in range(1, 2 * NZ):
        total = total + st_recv[i].astype(F32)
    tot_send[...] = total
    tot_copies = []
    for i in range(1, NX):
        copy = remote(tot_send, tot_recv.at[i - 1], tot_ssem.at[i - 1], tot_rsem.at[i - 1], dev(x + i, z, core))
        copy.start()
        tot_copies.append(copy)
    for copy in tot_copies:
        copy.wait()
    running = jnp.zeros((16, 128), F32)
    for i in range(1, NX):
        running = running + jnp.where(x - i >= 0, tot_recv[i - 1], 0.0)
    for i in range(2 * NZ):
        pre_send[i] = running.astype(BF16)
        running = running + st_recv[i].astype(F32)
    pre_copies = []
    for i in range(1, 2 * NZ):
        pos = lax.rem(row_pos + i, 2 * NZ)
        copy = remote(
            pre_send.at[pos], pre_recv.at[core, z], pre_ssem.at[i - 1], pre_rsem.at[i - 1], {"seq": x * 2 * NZ + pos}
        )
        copy.start()
        pre_copies.append(copy)
    pre_recv[core, z] = pre_send[row_pos]
    for copy in pre_copies:
        copy.wait()

    for n in range(2):
        for g in range(KV_HEADS):
            state = pre_recv[g].reshape(128, 128)
            values = lv[n * 128 : n * 128 + 128, g * 128 : g * 128 + 128]
            if n == 0:
                mix = dot(
                    jnp.concatenate([stacked(n, g), lin_scores[n, g]], axis=1), jnp.concatenate([state, values], axis=0)
                )
            else:
                qs = stacked(n, g)
                mix = dot(
                    jnp.concatenate([qs, qs, lin_scores[n, g]], axis=1),
                    jnp.concatenate([state, block0[g], values], axis=0),
                )
            mix = mix * lax.rsqrt(jnp.mean(mix * mix, axis=-1, keepdims=True) + EPSILON)
            for h in range(PER_GROUP):
                cols = slice((g * PER_GROUP + h) * 128, (g * PER_GROUP + h) * 128 + 128)
                normed[n * 128 : n * 128 + 128, cols] = (mix[h * 128 : h * 128 + 128] * lin_gain[:, cols]).astype(BF16)

    loads[3].wait()
    loads[4].wait()
    squares = jnp.zeros((TOK, 128), F32)
    for t in range(4):
        cols = slice(t * 512, t * 512 + 512)
        res = (hidden[:, cols].astype(F32) + dot(normed[...], wo[:, cols])).astype(BF16)
        resid[:, cols] = res
        wide = res.astype(F32)
        wide = wide * wide
        for s in range(4):
            squares = squares + wide[:, s * 128 : s * 128 + 128]
    factor = lax.rsqrt(jnp.sum(squares, axis=-1, keepdims=True) * (1.0 / D) + EPSILON)
    for t in range(4):
        cols = slice(t * 512, t * 512 + 512)
        layer_in[:, cols] = (resid[:, cols].astype(F32) * factor * soft_gain[:, cols]).astype(BF16)

    for i in range(5, 9):
        loads[i].wait()
    tables = [t.reshape(NX * NZ * CHIP_TOK, 128) for t in (key_table, value_table)]
    my_rows = pl.ds(pl.multiple_of(me * TOK, TOK), TOK)
    sib_copies = []
    for tensor in range(2):
        kv_send[tensor] = dot(layer_in[...], wkv[1, :, tensor * 128 : tensor * 128 + 128]).astype(BF16)
        copy = remote(kv_send.at[tensor], tables[tensor].at[my_rows], sib_ssem.at[tensor], sib_rsem.at[tensor], sibling)
        copy.start()
        sib_copies.append(copy)
    for tensor in range(2):
        tables[tensor][my_rows] = dot(layer_in[...], wkv[0, :, tensor * 128 : tensor * 128 + 128]).astype(BF16)
    for copy in sib_copies:
        copy.wait()

    started, landed = {}, set()
    sems = {"a1": (a1_ssem, a1_rsem), "a2": (a2_ssem, a2_rsem), "b1": (b1_ssem, b1_rsem), "b2": (b2_ssem, b2_rsem)}

    def launch(copy):
        kind, tensor, rest = copy[0], copy[1], copy[2:]

        def hop(direction, distance):
            return (-sign if direction == 0 else sign) * distance

        sx, sz = x, z
        if kind == "a1":
            index, to = (rest[0] - 1,), dev(x + rest[0], z, core)
        elif kind == "b1":
            sz, index = z + hop(rest[0], rest[1] - 1), (rest[0], rest[1] - 1)
            to = dev(x, z - hop(rest[0], 1), core)
        elif kind == "a2":
            sx, sz, index = x - rest[2], z + hop(rest[0], rest[1] - 1), (rest[0], rest[1] - 1, rest[2])
            to = dev(x, z - hop(rest[0], 1), core)
        else:
            r, j = rest
            sz, index = z + hop(*ORDER[r]), (r, j)
            along = (sign, -sign)[j if j < 2 else r % 2]
            if j == 2:
                sx = x - along
            to = dev(x + along, z, core)
        first, count = (0, ROWS_A) if kind in ("a1", "a2") else (ROWS_A, ROWS_B)
        src = lax.rem(sx + 2 * NX, NX) * NZ + lax.rem(sz + 2 * NZ, NZ)
        part = tables[tensor].at[pl.ds(pl.multiple_of(src * CHIP_TOK + first, 16), count)]
        ssem, rsem = sems[kind]
        started[copy] = remote(part, part, ssem.at[(tensor, *index)], rsem.at[(tensor, *index)], to)
        started[copy].start()

    def land(copy):
        if copy not in landed:
            landed.add(copy)
            started[copy].wait_recv()

    order = plan()
    missing = {copy for copy, _, _ in order if copy[1] == 0}
    first_wait = next(i for i, (_, needs, _) in enumerate(order) if needs is not None)
    for copy, _, _ in order[:first_wait]:
        launch(copy)

    loads[9].wait()
    loads[10].wait()

    def put_queries(part, write):
        q = dot(layer_in[...], wq[part]).astype(BF16)
        for n in range(2):
            for h in range(PER_GROUP):
                write(n, h, q[n * 128 : n * 128 + 128, h * 128 : h * 128 + 128])

    def write_send(n, h, value):
        q_send[n, h * 128 : h * 128 + 128, :] = value

    def write_own(n, h, value):
        q_all[core * 2 + n, h * 128 : h * 128 + 128, :] = value

    put_queries(1, write_send)
    q_copy = remote(q_send, q_all.at[pl.ds(core * 2, 2)], sib_ssem.at[2], sib_rsem.at[2], sibling)
    q_copy.start()
    put_queries(0, write_own)

    def find_repeats(i, carry):
        entries = [pattern_t[j, core, chip * 4 + i] for j in range(SEL)]
        for j in range(SEL):
            value = jnp.float32(0.0)
            for e in range(j):
                value = jnp.where(entries[e] == entries[j], jnp.float32(NEG), value)
            bias[i, j] = value
        return carry

    lax.fori_loop(0, 4, find_repeats, 0)

    def block_of(i, j):
        return pattern_t[j, core, chip * 4 + i]

    def score(i, pairs):
        q = q_all[i]
        best = None if pairs[0] == 0 else top[...]
        for p in pairs:
            keys = jnp.concatenate([key_table[block_of(i, 2 * p)], key_table[block_of(i, 2 * p + 1)]], axis=0)
            s = dot_nt(q, keys) * COEF
            left, right = s[:, 0:128] + bias[i, 2 * p], s[:, 128:256] + bias[i, 2 * p + 1]
            if p == 0:
                left = jnp.where(tri4, left, NEG)
            scores[p, :, 0:128] = left
            scores[p, :, 128:256] = right
            both = jnp.maximum(left, right)
            best = both if best is None else jnp.maximum(best, both)
        if pairs[-1] == PAIRS - 1:
            best = jnp.broadcast_to(jnp.max(best, axis=-1, keepdims=True), (512, 128))
        top[...] = best

    def weigh(i, pairs):
        total = None if pairs[0] == 0 else norms[i]
        for p in pairs:
            left = jnp.exp2(scores[p, :, 0:128] - top[...])
            right = jnp.exp2(scores[p, :, 128:256] - top[...])
            probs[i, :, p * 256 : p * 256 + 128] = left.astype(BF16)
            probs[i, :, p * 256 + 128 : p * 256 + 256] = right.astype(BF16)
            total = left + right if total is None else total + (left + right)
        if pairs[-1] == PAIRS - 1:
            total = jnp.broadcast_to(1.0 / jnp.sum(total, axis=-1, keepdims=True), (512, 128))
        norms[i] = total

    thirds = [range(0, 3), range(3, 6), range(6, 9)]
    work = [(f, i, pairs) for i in range(4) for f in (score, weigh) for pairs in thirds]
    work.reverse()

    for copy, needs, starts in order[first_wait:]:
        if needs is not None:
            land(needs)
            missing.discard(needs)
        if starts:
            launch(copy)
        if not missing and work:
            if len(work) == 24:
                q_copy.wait()
            part, i, pairs = work.pop()
            part(i, pairs)
    for copy in started.values():
        copy.wait_send()

    def attend(part, n):
        i = (1 - core if part == 0 else core) * 2 + n
        values = jnp.concatenate([value_table[block_of(i, j)] for j in range(SEL)], axis=0)
        out = dot(probs[i], values)
        rows = pl.ds(pl.multiple_of(n * 128, 128), 128)
        for h in range(PER_GROUP):
            value = (out[h * 128 : h * 128 + 128] * norms[i, h * 128 : h * 128 + 128, :]).astype(BF16)
            if part == 0:
                o_send[rows, h * 128 : h * 128 + 128] = value
            else:
                o_all[core, rows, h * 128 : h * 128 + 128] = value

    @pl.loop(0, 2)
    def _(n):
        attend(0, n)

    o_copy = remote(o_send, o_all.at[core], sib_ssem.at[3], sib_rsem.at[3], sibling)
    o_copy.start()

    @pl.loop(0, 2)
    def _(n):
        attend(1, n)

    o_copy.wait()
    o_ref[:, 0:512] = o_all[0]
    o_ref[:, 512:1024] = o_all[1]


def local(hidden_in, lin_query, lin_key, lin_value, lin_gain, lin_out_weight, soft_gain, soft_wq, soft_wk, soft_wv, pattern):
    dma = pltpu.SemaphoreType.DMA
    vmem, anywhere = pl.BlockSpec(memory_space=pltpu.VMEM), pl.BlockSpec(memory_space=pl.ANY)
    scratch = [
        pltpu.VMEM((TOK, D), BF16),
        pltpu.VMEM((TOK, 1024), BF16),
        pltpu.VMEM((TOK, 256), BF16),
        pltpu.VMEM((TOK, 256), BF16),
        pltpu.VMEM((1024, D), BF16),
        pltpu.VMEM((2, D, 512), BF16),
        pltpu.VMEM((2, D, 256), BF16),
        pltpu.VMEM((2, NZ, 16, 128), BF16),
        pltpu.VMEM((2 * NZ, 16, 128), BF16),
        pltpu.VMEM((16, 128), F32),
        pltpu.VMEM((NX - 1, 16, 128), F32),
        pltpu.VMEM((2 * NZ, 16, 128), BF16),
        pltpu.VMEM((2, NZ, 16, 128), BF16),
        pltpu.VMEM((2, 128, 128), BF16),
        pltpu.VMEM((2, 2, 512, 128), BF16),
        pltpu.VMEM((TOK, 1024), BF16),
        pltpu.VMEM((TOK, D), BF16),
        pltpu.VMEM((TOK, D), BF16),
        pltpu.VMEM((2, TOK, 128), BF16),
        pltpu.VMEM((2, 512, 128), BF16),
        pltpu.VMEM((4, 512, 128), BF16),
        pltpu.VMEM((NX * NZ * CHIP_TOK // BLOCK, BLOCK, 128), BF16),
        pltpu.VMEM((NX * NZ * CHIP_TOK // BLOCK, BLOCK, 128), BF16),
        pltpu.VMEM((PAIRS, 512, 256), F32),
        pltpu.VMEM((4, 512, SEL * BLOCK), BF16),
        pltpu.VMEM((512, 128), F32),
        pltpu.VMEM((4, 512, 128), F32),
        pltpu.SMEM((4, SEL), F32),
        pltpu.VMEM((TOK, 512), BF16),
        pltpu.VMEM((2, TOK, 512), BF16),
        dma((11,)),
        dma((2 * NZ - 1,)), dma((2 * NZ - 1,)),
        dma((NX - 1,)), dma((NX - 1,)),
        dma((2 * NZ - 1,)), dma((2 * NZ - 1,)),
        dma((4,)), dma((4,)),
        dma((2, NX - 1)), dma((2, NX - 1)),
        dma((2, 2, 4, NX)), dma((2, 2, 4, NX)),
        dma((2, 2, 4)), dma((2, 2, 4)),
        dma((2, NZ, 3)), dma((2, NZ, 3)),
    ]
    return pl.pallas_call(
        kernel,
        name="mixer_and_attention",
        out_shape=jax.ShapeDtypeStruct((TOK, 1024), BF16),
        in_specs=[pl.BlockSpec(memory_space=pltpu.SMEM), vmem, vmem] + [anywhere] * 8,
        out_specs=vmem,
        scratch_shapes=scratch,
        compiler_params=pltpu.CompilerParams(collective_id=0, has_side_effects=True, vmem_limit_bytes=56 << 20),
    )(
        pattern.transpose(2, 0, 1), lin_gain.reshape(1, 1024), soft_gain.reshape(1, D),
        hidden_in, lin_query, lin_key, lin_value, lin_out_weight, soft_wq, soft_wk, soft_wv,
    )


def solution(mesh):
    whole, split = P(), P(("dp", "seq"), None)
    in_specs = (split, split, split, split) + (whole,) * 7
    return jax.shard_map(local, mesh=mesh, in_specs=in_specs, out_specs=split, check_vma=False)
```

```python
import heapq
import math

import jax
import jax.numpy as jnp
from jax import lax
from jax.experimental import pallas as pl
from jax.experimental.pallas import tpu as pltpu
from jax.sharding import PartitionSpec as P

HEAD_DIM = 128
HEADS = 8
KV_HEADS = 2
PER_GROUP = HEADS // KV_HEADS
BLOCK = 128
SEL = 18
TOK = 256
D = 2048
NX, NZ = 4, 8
CHIP_TOK = 2 * TOK
PAIRS = SEL // 2
EPSILON = 1e-06
NEG = -1e30
COEF = HEAD_DIM ** (-0.5) * math.log2(math.e)
F32, BF16 = jnp.float32, jnp.bfloat16
MESH = pl.DeviceIdType.MESH

ROWS_A = 208
ROWS_B = CHIP_TOK - ROWS_A
FAR_FIRST = sorted(range(1, 2 * NZ), key=lambda i: -min(i, 2 * NZ - i))
ORDER = [(0, 0), (0, 1), (1, 1), (0, 2), (1, 2), (0, 3), (1, 3), (0, 4)]
STEPS = (4, 3)
LINK, LATENCY_US, SIBLING_US = 95000.0, 5.0, 3.0


def plan():
    ready, free, events, arrived, order = {"x": [], "z": []}, {"x": 0.0, "z": 0.0}, [], {}, []

    def add(copy, needs):
        kind, tensor = copy[:2]
        rank = (tensor, ("a1", "b1", "b2", "a2").index(kind), copy[3:] + copy[2:3] if kind in ("b1", "a2") else copy[2:])
        heapq.heappush(ready["x" if kind in ("a1", "b2") else "z"], (rank, copy, needs))

    def react(copy):
        kind, tensor, rest = copy[0], copy[1], copy[2:]
        if kind == "sib":
            for i in range(2):
                add(("b1", tensor, i, 1), copy)
                add(("b2", tensor, 0, i), copy)
        elif kind == "a1":
            add(("a2", tensor, 0, 1, rest[0]), copy)
            add(("a2", tensor, 1, 1, rest[0]), copy)
        elif kind == "b1":
            direction, step = rest
            if step < STEPS[direction]:
                add(("b1", tensor, direction, step + 1), copy)
            add(("b2", tensor, ORDER.index(rest), 0), copy)
            add(("b2", tensor, ORDER.index(rest), 1), copy)
        elif kind == "b2":
            if rest[1] == rest[0] % 2:
                add(("b2", tensor, rest[0], 2), copy)
        elif rest[1] < STEPS[rest[0]]:
            add(("a2", tensor, rest[0], rest[1] + 1, rest[2]), copy)

    for tensor in range(2):
        for i in (1, 3, 2):
            add(("a1", tensor, i), None)
        for i in range(2):
            add(("a2", tensor, i, 1, 0), None)
        heapq.heappush(events, (SIBLING_US + 0.5 * tensor, tensor, ("sib", tensor)))
    now, count = 0.0, 2
    while True:
        for link in "xz":
            if free[link] <= now and ready[link]:
                _, copy, needs = heapq.heappop(ready[link])
                order.append((now, copy, needs, True))
                rows = (ROWS_A if copy[0] in ("a1", "a2") else ROWS_B) * (2 if copy[0] == "a1" and copy[2] == 2 else 1)
                free[link] = now + rows * 256 / LINK
                arrived[copy] = free[link] + LATENCY_US
                order.append((arrived[copy], copy, copy, False))
                for event in ((arrived[copy], count, copy), (free[link], count + 1, None)):
                    heapq.heappush(events, event)
                count += 2
        if not events:
            return [step[1:] for step in sorted(order, key=lambda step: step[0])]
        now, _, copy = heapq.heappop(events)
        if copy:
            react(copy)


def dot(a, b):
    return jnp.dot(a, b, preferred_element_type=F32)


def dot_nt(a, b):
    return lax.dot_general(a, b, (((1,), (1,)), ((), ())), preferred_element_type=F32)


def dot_tn(a, b):
    return lax.dot_general(a, b, (((0,), (0,)), ((), ())), preferred_element_type=F32)


def kernel(
    pattern_t, lin_gain, soft_gain, hidden_hbm, lq_hbm, lk_hbm, lv_hbm, wo_hbm, wq_hbm, wk_hbm, wv_hbm,
    o_ref,
    hidden, lq, lk, lv, wo, wq, wkv, st_send, st_recv, tot_send, tot_recv, pre_send, pre_recv,
    block0, lin_scores, normed, resid, layer_in, kv_send, q_send, q_all, key_table, value_table, scores, probs, top, norms, bias,
    o_send, o_all,
    load_sem, st_ssem, st_rsem, tot_ssem, tot_rsem, pre_ssem, pre_rsem, sib_ssem, sib_rsem,
    a1_ssem, a1_rsem, a2_ssem, a2_rsem, b1_ssem, b1_rsem, b2_ssem, b2_rsem,
):
    me = lax.axis_index("seq")
    core = lax.rem(me, 2)
    chip = me // 2
    z = lax.rem(chip, NZ)
    x = chip // NZ
    sign = 1 - 2 * core
    row_pos = z * 2 + core

    def dev(cx, cz, cc):
        return {"seq": (lax.rem(cx + 2 * NX, NX) * NZ + lax.rem(cz + 2 * NZ, NZ)) * 2 + cc}

    sibling = dev(x, z, 1 - core)

    def remote(src, dst, ssem, rsem, device):
        return pltpu.make_async_remote_copy(
            src_ref=src, dst_ref=dst, send_sem=ssem, recv_sem=rsem, device_id=device, device_id_type=MESH
        )

    own_q = pl.ds(pl.multiple_of(core * 512, 512), 512)
    sib_q = pl.ds(pl.multiple_of((1 - core) * 512, 512), 512)
    own_h = pl.ds(pl.multiple_of(core * 128, 128), 128)
    sib_h = pl.ds(pl.multiple_of((1 - core) * 128, 128), 128)
    loads = [
        (lk_hbm, lk),
        (lv_hbm, lv),
        (lq_hbm, lq),
        (wo_hbm, wo),
        (hidden_hbm, hidden),
        (wk_hbm.at[:, own_h], wkv.at[0, :, 0:128]),
        (wv_hbm.at[:, own_h], wkv.at[0, :, 128:256]),
        (wk_hbm.at[:, sib_h], wkv.at[1, :, 0:128]),
        (wv_hbm.at[:, sib_h], wkv.at[1, :, 128:256]),
        (wq_hbm.at[:, own_q], wq.at[0]),
        (wq_hbm.at[:, sib_q], wq.at[1]),
    ]
    loads = [pltpu.make_async_copy(src, dst, load_sem.at[i]) for i, (src, dst) in enumerate(loads)]
    for copy in loads[:3]:
        copy.start()

    barrier = pltpu.get_barrier_semaphore()
    for i in FAR_FIRST:
        pos = lax.rem(row_pos + i, 2 * NZ)
        pl.semaphore_signal(barrier, inc=1, device_id={"seq": x * 2 * NZ + pos}, device_id_type=MESH)
    for i in range(1, NX):
        pl.semaphore_signal(barrier, inc=1, device_id=dev(x + i, z, core), device_id_type=MESH)

    loads[0].wait()
    loads[1].wait()

    for g in range(KV_HEADS):
        cols = slice(g * 128, g * 128 + 128)
        first = dot_tn(lk[0:128, cols], lv[0:128, cols])
        second = dot_tn(lk[128:256, cols], lv[128:256, cols])
        block0[g] = first.astype(BF16)
        st_send[g] = (first + second).astype(BF16).reshape(NZ, 16, 128)

    pl.semaphore_wait(barrier, 2 * NZ - 1 + NX - 1)

    st_copies = []
    for i in FAR_FIRST:
        pos = lax.rem(row_pos + i, 2 * NZ)
        copy = remote(
            st_send.at[lax.rem(pos, 2), pos // 2], st_recv.at[row_pos], st_ssem.at[i - 1], st_rsem.at[i - 1],
            {"seq": x * 2 * NZ + pos},
        )
        copy.start()
        st_copies.append(copy)
    for copy in loads[3:]:
        copy.start()
    st_recv[row_pos] = st_send[core, z]

    loads[2].wait()
    tri = lax.broadcasted_iota(jnp.int32, (128, 128), 0) >= lax.broadcasted_iota(jnp.int32, (128, 128), 1)
    tri4 = jnp.concatenate([tri] * PER_GROUP, axis=0)

    def stacked(n, g):
        return jnp.concatenate(
            [lq[n * 128 : n * 128 + 128, (g * PER_GROUP + h) * 128 : (g * PER_GROUP + h) * 128 + 128] for h in range(PER_GROUP)],
            axis=0,
        )

    for n in range(2):
        for g in range(KV_HEADS):
            keys = lk[n * 128 : n * 128 + 128, g * 128 : g * 128 + 128]
            lin_scores[n, g] = jnp.where(tri4, dot_nt(stacked(n, g), keys), 0.0).astype(BF16)

    for copy in st_copies:
        copy.wait_recv()
    total = st_recv[0].astype(F32)
    for i in range(1, 2 * NZ):
        total = total + st_recv[i].astype(F32)
    tot_send[...] = total
    tot_copies = []
    for i in range(1, NX):
        copy = remote(tot_send, tot_recv.at[i - 1], tot_ssem.at[i - 1], tot_rsem.at[i - 1], dev(x + i, z, core))
        copy.start()
        tot_copies.append(copy)
    for copy in tot_copies:
        copy.wait_recv()
    running = jnp.zeros((16, 128), F32)
    for i in range(1, NX):
        running = running + jnp.where(x - i >= 0, tot_recv[i - 1], 0.0)
    for i in range(2 * NZ):
        pre_send[i] = running.astype(BF16)
        running = running + st_recv[i].astype(F32)
    pre_copies = []
    for i in FAR_FIRST:
        pos = lax.rem(row_pos + i, 2 * NZ)
        copy = remote(
            pre_send.at[pos], pre_recv.at[core, z], pre_ssem.at[i - 1], pre_rsem.at[i - 1], {"seq": x * 2 * NZ + pos}
        )
        copy.start()
        pre_copies.append(copy)
    pre_recv[core, z] = pre_send[row_pos]
    for copy in pre_copies:
        copy.wait_recv()

    for n in range(2):
        for g in range(KV_HEADS):
            state = pre_recv[g].reshape(128, 128)
            values = lv[n * 128 : n * 128 + 128, g * 128 : g * 128 + 128]
            if n == 0:
                mix = dot(
                    jnp.concatenate([stacked(n, g), lin_scores[n, g]], axis=1), jnp.concatenate([state, values], axis=0)
                )
            else:
                qs = stacked(n, g)
                mix = dot(
                    jnp.concatenate([qs, qs, lin_scores[n, g]], axis=1),
                    jnp.concatenate([state, block0[g], values], axis=0),
                )
            mix = mix * lax.rsqrt(jnp.mean(mix * mix, axis=-1, keepdims=True) + EPSILON)
            for h in range(PER_GROUP):
                cols = slice((g * PER_GROUP + h) * 128, (g * PER_GROUP + h) * 128 + 128)
                normed[n * 128 : n * 128 + 128, cols] = (mix[h * 128 : h * 128 + 128] * lin_gain[:, cols]).astype(BF16)

    loads[3].wait()
    loads[4].wait()
    squares = jnp.zeros((TOK, 128), F32)
    for t in range(4):
        cols = slice(t * 512, t * 512 + 512)
        res = (hidden[:, cols].astype(F32) + dot(normed[...], wo[:, cols])).astype(BF16)
        resid[:, cols] = res
        wide = res.astype(F32)
        wide = wide * wide
        for s in range(4):
            squares = squares + wide[:, s * 128 : s * 128 + 128]
    factor = lax.rsqrt(jnp.sum(squares, axis=-1, keepdims=True) * (1.0 / D) + EPSILON)
    for t in range(4):
        cols = slice(t * 512, t * 512 + 512)
        layer_in[:, cols] = (resid[:, cols].astype(F32) * factor * soft_gain[:, cols]).astype(BF16)

    for i in range(5, 9):
        loads[i].wait()
    tables = [t.reshape(NX * NZ * CHIP_TOK, 128) for t in (key_table, value_table)]
    my_rows = pl.ds(pl.multiple_of(me * TOK, TOK), TOK)
    sib_copies = []
    both = dot(layer_in[...], wkv[1]).astype(BF16)
    for tensor in range(2):
        kv_send[tensor] = both[:, tensor * 128 : tensor * 128 + 128]
        copy = remote(kv_send.at[tensor], tables[tensor].at[my_rows], sib_ssem.at[tensor], sib_rsem.at[tensor], sibling)
        copy.start()
        sib_copies.append(copy)
    both = dot(layer_in[...], wkv[0]).astype(BF16)
    for tensor in range(2):
        tables[tensor][my_rows] = both[:, tensor * 128 : tensor * 128 + 128]

    started, landed = {}, set()
    sems = {"a1": (a1_ssem, a1_rsem), "a2": (a2_ssem, a2_rsem), "b1": (b1_ssem, b1_rsem), "b2": (b2_ssem, b2_rsem)}

    def launch(copy):
        kind, tensor, rest = copy[0], copy[1], copy[2:]

        def hop(direction, distance):
            return (-sign if direction == 0 else sign) * distance

        sx, sz = x, z
        if kind == "a1":
            index, to = (rest[0] - 1,), dev(x + rest[0], z, core)
        elif kind == "b1":
            sz, index = z + hop(rest[0], rest[1] - 1), (rest[0], rest[1] - 1)
            to = dev(x, z - hop(rest[0], 1), core)
        elif kind == "a2":
            sx, sz, index = x - rest[2], z + hop(rest[0], rest[1] - 1), (rest[0], rest[1] - 1, rest[2])
            to = dev(x, z - hop(rest[0], 1), core)
        else:
            r, j = rest
            sz, index = z + hop(*ORDER[r]), (r, j)
            along = (sign, -sign)[j if j < 2 else r % 2]
            if j == 2:
                sx = x - along
            to = dev(x + along, z, core)
        if kind in ("a1", "a2"):
            first, count = core * ROWS_B, ROWS_A
        else:
            first, count = (1 - core) * ROWS_A, ROWS_B
        src = lax.rem(sx + 2 * NX, NX) * NZ + lax.rem(sz + 2 * NZ, NZ)
        part = tables[tensor].at[pl.ds(pl.multiple_of(src * CHIP_TOK + first, 16), count)]
        ssem, rsem = sems[kind]
        started[copy] = remote(part, part, ssem.at[(tensor, *index)], rsem.at[(tensor, *index)], to)
        started[copy].start()

    def land(copy):
        if copy not in landed:
            landed.add(copy)
            (sib_copies[copy[1]] if copy[0] == "sib" else started[copy]).wait_recv()

    order = plan()
    missing = {copy for copy, _, _ in order if copy[1] == 0}
    loads[9].wait()
    loads[10].wait()

    def put_queries(part, write):
        q = dot(layer_in[...], wq[part]).astype(BF16)
        for n in range(2):
            for h in range(PER_GROUP):
                write(n, h, q[n * 128 : n * 128 + 128, h * 128 : h * 128 + 128])

    def write_send(n, h, value):
        q_send[n, h * 128 : h * 128 + 128, :] = value

    def write_own(n, h, value):
        q_all[core * 2 + n, h * 128 : h * 128 + 128, :] = value

    q_copy = remote(q_send, q_all.at[pl.ds(core * 2, 2)], sib_ssem.at[2], sib_rsem.at[2], sibling)

    def block_of(i, j):
        return pattern_t[j, core, chip * 4 + i]

    def score(i, pairs):
        q = q_all[i]
        best = None if pairs[0] == 0 else top[...]
        for p in pairs:
            keys = jnp.concatenate([key_table[block_of(i, 2 * p)], key_table[block_of(i, 2 * p + 1)]], axis=0)
            s = dot_nt(q, keys) * COEF
            left, right = s[:, 0:128] + bias[i, 2 * p], s[:, 128:256] + bias[i, 2 * p + 1]
            if p == 0:
                left = jnp.where(tri4, left, NEG)
            scores[p, :, 0:128] = left
            scores[p, :, 128:256] = right
            both = jnp.maximum(left, right)
            best = both if best is None else jnp.maximum(best, both)
        if pairs[-1] == PAIRS - 1:
            best = jnp.broadcast_to(jnp.max(best, axis=-1, keepdims=True), (512, 128))
        top[...] = best

    def weigh(i, pairs):
        total = None if pairs[0] == 0 else norms[i]
        for p in pairs:
            left = jnp.exp2(scores[p, :, 0:128] - top[...])
            right = jnp.exp2(scores[p, :, 128:256] - top[...])
            probs[i, :, p * 256 : p * 256 + 128] = left.astype(BF16)
            probs[i, :, p * 256 + 128 : p * 256 + 256] = right.astype(BF16)
            total = left + right if total is None else total + (left + right)
        if pairs[-1] == PAIRS - 1:
            total = jnp.broadcast_to(1.0 / jnp.sum(total, axis=-1, keepdims=True), (512, 128))
        norms[i] = total

    thirds = [range(0, 3), range(3, 6), range(6, 9)]
    work = [(f, i, pairs) for i in range(4) for f in (score, weigh) for pairs in thirds]
    work.reverse()

    def find_repeats(i, carry):
        entries = [pattern_t[j, core, chip * 4 + i] for j in range(SEL)]
        for j in range(SEL):
            value = jnp.float32(0.0)
            for e in range(j):
                value = jnp.where(entries[e] == entries[j], jnp.float32(NEG), value)
            bias[i, j] = value
        return carry


    waits = 0
    for copy, needs, starts in order:
        if needs is not None:
            if needs not in landed and waits == 0:
                put_queries(1, write_send)
                q_copy.start()
                waits = 1
            elif needs not in landed and waits == 1 and needs[0] != "sib":
                put_queries(0, write_own)
                lax.fori_loop(0, 4, find_repeats, 0)
                waits = 2
            land(needs)
            missing.discard(needs)
        if starts:
            launch(copy)
        if not missing and work:
            if len(work) == 24:
                q_copy.wait()
            part, i, pairs = work.pop()
            part(i, pairs)
    while work:
        part, i, pairs = work.pop()
        part(i, pairs)

    def attend(part, n):
        i = (1 - core if part == 0 else core) * 2 + n
        values = jnp.concatenate([value_table[block_of(i, j)] for j in range(SEL)], axis=0)
        out = dot(probs[i], values)
        rows = pl.ds(pl.multiple_of(n * 128, 128), 128)
        for h in range(PER_GROUP):
            value = (out[h * 128 : h * 128 + 128] * norms[i, h * 128 : h * 128 + 128, :]).astype(BF16)
            if part == 0:
                o_send[rows, h * 128 : h * 128 + 128] = value
            else:
                o_all[core, rows, h * 128 : h * 128 + 128] = value

    @pl.loop(0, 2)
    def _(n):
        attend(0, n)

    o_copy = remote(o_send, o_all.at[core], sib_ssem.at[3], sib_rsem.at[3], sibling)
    o_copy.start()

    @pl.loop(0, 2)
    def _(n):
        attend(1, n)

    for copy in [*st_copies, *tot_copies, *pre_copies, *sib_copies, *started.values()]:
        copy.wait_send()
    o_copy.wait()
    o_ref[:, 0:512] = o_all[0]
    o_ref[:, 512:1024] = o_all[1]


def local(hidden_in, lin_query, lin_key, lin_value, lin_gain, lin_out_weight, soft_gain, soft_wq, soft_wk, soft_wv, pattern):
    dma = pltpu.SemaphoreType.DMA
    vmem, anywhere = pl.BlockSpec(memory_space=pltpu.VMEM), pl.BlockSpec(memory_space=pl.ANY)
    scratch = [
        pltpu.VMEM((TOK, D), BF16),
        pltpu.VMEM((TOK, 1024), BF16),
        pltpu.VMEM((TOK, 256), BF16),
        pltpu.VMEM((TOK, 256), BF16),
        pltpu.VMEM((1024, D), BF16),
        pltpu.VMEM((2, D, 512), BF16),
        pltpu.VMEM((2, D, 256), BF16),
        pltpu.VMEM((2, NZ, 16, 128), BF16),
        pltpu.VMEM((2 * NZ, 16, 128), BF16),
        pltpu.VMEM((16, 128), F32),
        pltpu.VMEM((NX - 1, 16, 128), F32),
        pltpu.VMEM((2 * NZ, 16, 128), BF16),
        pltpu.VMEM((2, NZ, 16, 128), BF16),
        pltpu.VMEM((2, 128, 128), BF16),
        pltpu.VMEM((2, 2, 512, 128), BF16),
        pltpu.VMEM((TOK, 1024), BF16),
        pltpu.VMEM((TOK, D), BF16),
        pltpu.VMEM((TOK, D), BF16),
        pltpu.VMEM((2, TOK, 128), BF16),
        pltpu.VMEM((2, 512, 128), BF16),
        pltpu.VMEM((4, 512, 128), BF16),
        pltpu.VMEM((NX * NZ * CHIP_TOK // BLOCK, BLOCK, 128), BF16),
        pltpu.VMEM((NX * NZ * CHIP_TOK // BLOCK, BLOCK, 128), BF16),
        pltpu.VMEM((PAIRS, 512, 256), F32),
        pltpu.VMEM((4, 512, SEL * BLOCK), BF16),
        pltpu.VMEM((512, 128), F32),
        pltpu.VMEM((4, 512, 128), F32),
        pltpu.SMEM((4, SEL), F32),
        pltpu.VMEM((TOK, 512), BF16),
        pltpu.VMEM((2, TOK, 512), BF16),
        dma((11,)),
        dma((2 * NZ - 1,)), dma((2 * NZ - 1,)),
        dma((NX - 1,)), dma((NX - 1,)),
        dma((2 * NZ - 1,)), dma((2 * NZ - 1,)),
        dma((4,)), dma((4,)),
        dma((2, NX - 1)), dma((2, NX - 1)),
        dma((2, 2, 4, NX)), dma((2, 2, 4, NX)),
        dma((2, 2, 4)), dma((2, 2, 4)),
        dma((2, NZ, 3)), dma((2, NZ, 3)),
    ]
    return pl.pallas_call(
        kernel,
        name="mixer_and_attention",
        out_shape=jax.ShapeDtypeStruct((TOK, 1024), BF16),
        in_specs=[pl.BlockSpec(memory_space=pltpu.SMEM), vmem, vmem] + [anywhere] * 8,
        out_specs=vmem,
        scratch_shapes=scratch,
        compiler_params=pltpu.CompilerParams(collective_id=0, has_side_effects=True, vmem_limit_bytes=56 << 20),
    )(
        pattern.transpose(2, 0, 1), lin_gain.reshape(1, 1024), soft_gain.reshape(1, D),
        hidden_in, lin_query, lin_key, lin_value, lin_out_weight, soft_wq, soft_wk, soft_wv,
    )


def solution(mesh):
    whole, split = P(), P(("dp", "seq"), None)
    in_specs = (split, split, split, split) + (whole,) * 7
    return jax.shard_map(local, mesh=mesh, in_specs=in_specs, out_specs=split, check_vma=False)
```

```python
import heapq
import math

import jax
import jax.numpy as jnp
from jax import lax
from jax.experimental import pallas as pl
from jax.experimental.pallas import tpu as pltpu
from jax.sharding import PartitionSpec as P

HEAD_DIM = 128
HEADS = 8
KV_HEADS = 2
PER_GROUP = HEADS // KV_HEADS
BLOCK = 128
SEL = 18
TOK = 256
D = 2048
NX, NZ = 4, 8
CHIP_TOK = 2 * TOK
PAIRS = SEL // 2
EPSILON = 1e-06
NEG = -1e30
COEF = HEAD_DIM ** (-0.5) * math.log2(math.e)
F32, BF16 = jnp.float32, jnp.bfloat16
MESH = pl.DeviceIdType.MESH

ROWS_A = 208
ROWS_B = CHIP_TOK - ROWS_A
FAR_FIRST = sorted(range(1, 2 * NZ), key=lambda i: -min(i, 2 * NZ - i))
ORDER = [(0, 0), (0, 1), (1, 1), (0, 2), (1, 2), (0, 3), (1, 3), (0, 4)]
STEPS = (4, 3)
LINK, LATENCY_US, SIBLING_US = 95000.0, 5.0, 3.0


def plan():
    ready, free, events, arrived, order = {"x": [], "z": []}, {"x": 0.0, "z": 0.0}, [], {}, []

    def add(copy, needs):
        kind, tensor = copy[:2]
        rank = (tensor, ("a1", "b1", "b2", "a2").index(kind), copy[3:] + copy[2:3] if kind in ("b1", "a2") else copy[2:])
        heapq.heappush(ready["x" if kind in ("a1", "b2") else "z"], (rank, copy, needs))

    def react(copy):
        kind, tensor, rest = copy[0], copy[1], copy[2:]
        if kind == "sib":
            for i in range(2):
                add(("b1", tensor, i, 1), copy)
                add(("b2", tensor, 0, i), copy)
        elif kind == "a1":
            add(("a2", tensor, 0, 1, rest[0]), copy)
            add(("a2", tensor, 1, 1, rest[0]), copy)
        elif kind == "b1":
            direction, step = rest
            if step < STEPS[direction]:
                add(("b1", tensor, direction, step + 1), copy)
            add(("b2", tensor, ORDER.index(rest), 0), copy)
            add(("b2", tensor, ORDER.index(rest), 1), copy)
        elif kind == "b2":
            if rest[1] == rest[0] % 2:
                add(("b2", tensor, rest[0], 2), copy)
        elif rest[1] < STEPS[rest[0]]:
            add(("a2", tensor, rest[0], rest[1] + 1, rest[2]), copy)

    for tensor in range(2):
        for i in (1, 3, 2):
            add(("a1", tensor, i), None)
        for i in range(2):
            add(("a2", tensor, i, 1, 0), None)
        heapq.heappush(events, (SIBLING_US + 0.5 * tensor, tensor, ("sib", tensor)))
    now, count = 0.0, 2
    while True:
        for link in "xz":
            if free[link] <= now and ready[link]:
                _, copy, needs = heapq.heappop(ready[link])
                order.append((now, copy, needs, True))
                rows = (ROWS_A if copy[0] in ("a1", "a2") else ROWS_B) * (2 if copy[0] == "a1" and copy[2] == 2 else 1)
                free[link] = now + rows * 256 / LINK
                arrived[copy] = free[link] + LATENCY_US
                order.append((arrived[copy], copy, copy, False))
                for event in ((arrived[copy], count, copy), (free[link], count + 1, None)):
                    heapq.heappush(events, event)
                count += 2
        if not events:
            return [step[1:] for step in sorted(order, key=lambda step: step[0])]
        now, _, copy = heapq.heappop(events)
        if copy:
            react(copy)


def dot(a, b):
    return jnp.dot(a, b, preferred_element_type=F32)


def dot_nt(a, b):
    return lax.dot_general(a, b, (((1,), (1,)), ((), ())), preferred_element_type=F32)


def dot_tn(a, b):
    return lax.dot_general(a, b, (((0,), (0,)), ((), ())), preferred_element_type=F32)


def kernel(
    pattern_hbm, lin_gain_hbm, soft_gain_hbm, hidden_hbm, lq_hbm, lk_hbm, lv_hbm, wo_hbm, wq_hbm, wk_hbm, wv_hbm,
    o_ref,
    hidden, lq, lk, lv, wo, wq, wkv, st_send, st_recv, tot_send, tot_recv, pre_send, pre_recv,
    block0, lin_scores, normed, resid, layer_in, kv_send, q_send, q_all, key_table, value_table, scores, probs, top, norms, bias,
    o_send, o_all,
    pattern_t, lin_gain, soft_gain,
    load_sem, st_ssem, st_rsem, tot_ssem, tot_rsem, pre_ssem, pre_rsem, sib_ssem, sib_rsem,
    a1_ssem, a1_rsem, a2_ssem, a2_rsem, b1_ssem, b1_rsem, b2_ssem, b2_rsem,
):
    me = lax.axis_index("seq")
    core = lax.rem(me, 2)
    chip = me // 2
    z = lax.rem(chip, NZ)
    x = chip // NZ
    sign = 1 - 2 * core
    row_pos = z * 2 + core

    def dev(cx, cz, cc):
        return {"seq": (lax.rem(cx + 2 * NX, NX) * NZ + lax.rem(cz + 2 * NZ, NZ)) * 2 + cc}

    sibling = dev(x, z, 1 - core)

    def remote(src, dst, ssem, rsem, device):
        return pltpu.make_async_remote_copy(
            src_ref=src, dst_ref=dst, send_sem=ssem, recv_sem=rsem, device_id=device, device_id_type=MESH
        )

    own_q = pl.ds(pl.multiple_of(core * 512, 512), 512)
    sib_q = pl.ds(pl.multiple_of((1 - core) * 512, 512), 512)
    own_h = pl.ds(pl.multiple_of(core * 128, 128), 128)
    sib_h = pl.ds(pl.multiple_of((1 - core) * 128, 128), 128)
    loads = [
        (lk_hbm, lk),
        (lv_hbm, lv),
        (lq_hbm, lq),
        (wo_hbm, wo),
        (hidden_hbm, hidden),
        (wk_hbm.at[:, own_h], wkv.at[0, :, 0:128]),
        (wv_hbm.at[:, own_h], wkv.at[0, :, 128:256]),
        (wk_hbm.at[:, sib_h], wkv.at[1, :, 0:128]),
        (wv_hbm.at[:, sib_h], wkv.at[1, :, 128:256]),
        (wq_hbm.at[:, own_q], wq.at[0]),
        (wq_hbm.at[:, sib_q], wq.at[1]),
        (lin_gain_hbm, lin_gain),
        (soft_gain_hbm, soft_gain),
        (pattern_hbm, pattern_t),
    ]
    loads = [pltpu.make_async_copy(src, dst, load_sem.at[i]) for i, (src, dst) in enumerate(loads)]
    for copy in loads[:3]:
        copy.start()

    barrier = pltpu.get_barrier_semaphore()
    for i in FAR_FIRST:
        pos = lax.rem(row_pos + i, 2 * NZ)
        pl.semaphore_signal(barrier, inc=1, device_id={"seq": x * 2 * NZ + pos}, device_id_type=MESH)
    for i in range(1, NX):
        pl.semaphore_signal(barrier, inc=1, device_id=dev(x + i, z, core), device_id_type=MESH)

    loads[0].wait()
    loads[1].wait()

    for g in range(KV_HEADS):
        cols = slice(g * 128, g * 128 + 128)
        first = dot_tn(lk[0:128, cols], lv[0:128, cols])
        second = dot_tn(lk[128:256, cols], lv[128:256, cols])
        block0[g] = first.astype(BF16)
        st_send[g] = (first + second).astype(BF16).reshape(NZ, 16, 128)

    pl.semaphore_wait(barrier, 2 * NZ - 1 + NX - 1)

    st_copies = []
    for i in FAR_FIRST:
        pos = lax.rem(row_pos + i, 2 * NZ)
        copy = remote(
            st_send.at[lax.rem(pos, 2), pos // 2], st_recv.at[row_pos], st_ssem.at[i - 1], st_rsem.at[i - 1],
            {"seq": x * 2 * NZ + pos},
        )
        copy.start()
        st_copies.append(copy)
    for copy in loads[3:]:
        copy.start()
    st_recv[row_pos] = st_send[core, z]

    loads[2].wait()
    tri = lax.broadcasted_iota(jnp.int32, (128, 128), 0) >= lax.broadcasted_iota(jnp.int32, (128, 128), 1)
    tri4 = jnp.concatenate([tri] * PER_GROUP, axis=0)

    def stacked(n, g):
        return jnp.concatenate(
            [lq[n * 128 : n * 128 + 128, (g * PER_GROUP + h) * 128 : (g * PER_GROUP + h) * 128 + 128] for h in range(PER_GROUP)],
            axis=0,
        )

    for n in range(2):
        for g in range(KV_HEADS):
            keys = lk[n * 128 : n * 128 + 128, g * 128 : g * 128 + 128]
            lin_scores[n, g] = jnp.where(tri4, dot_nt(stacked(n, g), keys), 0.0).astype(BF16)

    for copy in st_copies:
        copy.wait_recv()
    total = st_recv[0].astype(F32)
    for i in range(1, 2 * NZ):
        total = total + st_recv[i].astype(F32)
    tot_send[...] = total
    tot_copies = []
    for i in range(1, NX):
        copy = remote(tot_send, tot_recv.at[i - 1], tot_ssem.at[i - 1], tot_rsem.at[i - 1], dev(x + i, z, core))
        copy.start()
        tot_copies.append(copy)
    for copy in tot_copies:
        copy.wait_recv()
    running = jnp.zeros((16, 128), F32)
    for i in range(1, NX):
        running = running + jnp.where(x - i >= 0, tot_recv[i - 1], 0.0)
    for i in range(2 * NZ):
        pre_send[i] = running.astype(BF16)
        running = running + st_recv[i].astype(F32)
    pre_copies = []
    for i in FAR_FIRST:
        pos = lax.rem(row_pos + i, 2 * NZ)
        copy = remote(
            pre_send.at[pos], pre_recv.at[core, z], pre_ssem.at[i - 1], pre_rsem.at[i - 1], {"seq": x * 2 * NZ + pos}
        )
        copy.start()
        pre_copies.append(copy)
    pre_recv[core, z] = pre_send[row_pos]
    for copy in pre_copies:
        copy.wait_recv()

    loads[11].wait()
    loads[12].wait()
    loads[13].wait()
    for n in range(2):
        for g in range(KV_HEADS):
            state = pre_recv[g].reshape(128, 128)
            values = lv[n * 128 : n * 128 + 128, g * 128 : g * 128 + 128]
            if n == 0:
                mix = dot(
                    jnp.concatenate([stacked(n, g), lin_scores[n, g]], axis=1), jnp.concatenate([state, values], axis=0)
                )
            else:
                qs = stacked(n, g)
                mix = dot(
                    jnp.concatenate([qs, qs, lin_scores[n, g]], axis=1),
                    jnp.concatenate([state, block0[g], values], axis=0),
                )
            mix = mix * lax.rsqrt(jnp.mean(mix * mix, axis=-1, keepdims=True) + EPSILON)
            for h in range(PER_GROUP):
                cols = slice((g * PER_GROUP + h) * 128, (g * PER_GROUP + h) * 128 + 128)
                normed[n * 128 : n * 128 + 128, cols] = (mix[h * 128 : h * 128 + 128] * lin_gain[:, cols]).astype(BF16)

    loads[3].wait()
    loads[4].wait()
    squares = jnp.zeros((TOK, 128), F32)
    for t in range(4):
        cols = slice(t * 512, t * 512 + 512)
        res = (hidden[:, cols].astype(F32) + dot(normed[...], wo[:, cols])).astype(BF16)
        resid[:, cols] = res
        wide = res.astype(F32)
        wide = wide * wide
        for s in range(4):
            squares = squares + wide[:, s * 128 : s * 128 + 128]
    factor = lax.rsqrt(jnp.sum(squares, axis=-1, keepdims=True) * (1.0 / D) + EPSILON)
    for t in range(4):
        cols = slice(t * 512, t * 512 + 512)
        layer_in[:, cols] = (resid[:, cols].astype(F32) * factor * soft_gain[:, cols]).astype(BF16)

    for i in range(5, 9):
        loads[i].wait()
    tables = [t.reshape(NX * NZ * CHIP_TOK, 128) for t in (key_table, value_table)]
    my_rows = pl.ds(pl.multiple_of(me * TOK, TOK), TOK)
    sib_copies = []
    both = dot(layer_in[...], wkv[1]).astype(BF16)
    for tensor in range(2):
        kv_send[tensor] = both[:, tensor * 128 : tensor * 128 + 128]
        copy = remote(kv_send.at[tensor], tables[tensor].at[my_rows], sib_ssem.at[tensor], sib_rsem.at[tensor], sibling)
        copy.start()
        sib_copies.append(copy)
    both = dot(layer_in[...], wkv[0]).astype(BF16)
    for tensor in range(2):
        tables[tensor][my_rows] = both[:, tensor * 128 : tensor * 128 + 128]

    started, landed = {}, set()
    sems = {"a1": (a1_ssem, a1_rsem), "a2": (a2_ssem, a2_rsem), "b1": (b1_ssem, b1_rsem), "b2": (b2_ssem, b2_rsem)}

    def launch(copy):
        kind, tensor, rest = copy[0], copy[1], copy[2:]

        def hop(direction, distance):
            return (-sign if direction == 0 else sign) * distance

        sx, sz = x, z
        if kind == "a1":
            index, to = (rest[0] - 1,), dev(x + rest[0], z, core)
        elif kind == "b1":
            sz, index = z + hop(rest[0], rest[1] - 1), (rest[0], rest[1] - 1)
            to = dev(x, z - hop(rest[0], 1), core)
        elif kind == "a2":
            sx, sz, index = x - rest[2], z + hop(rest[0], rest[1] - 1), (rest[0], rest[1] - 1, rest[2])
            to = dev(x, z - hop(rest[0], 1), core)
        else:
            r, j = rest
            sz, index = z + hop(*ORDER[r]), (r, j)
            along = (sign, -sign)[j if j < 2 else r % 2]
            if j == 2:
                sx = x - along
            to = dev(x + along, z, core)
        if kind in ("a1", "a2"):
            first, count = core * ROWS_B, ROWS_A
        else:
            first, count = (1 - core) * ROWS_A, ROWS_B
        src = lax.rem(sx + 2 * NX, NX) * NZ + lax.rem(sz + 2 * NZ, NZ)
        part = tables[tensor].at[pl.ds(pl.multiple_of(src * CHIP_TOK + first, 16), count)]
        ssem, rsem = sems[kind]
        started[copy] = remote(part, part, ssem.at[(tensor, *index)], rsem.at[(tensor, *index)], to)
        started[copy].start()

    def land(copy):
        if copy not in landed:
            landed.add(copy)
            (sib_copies[copy[1]] if copy[0] == "sib" else started[copy]).wait_recv()

    order = plan()
    missing = {copy for copy, _, _ in order if copy[1] == 0}
    loads[9].wait()
    loads[10].wait()

    def put_queries(part, write):
        q = dot(layer_in[...], wq[part]).astype(BF16)
        for n in range(2):
            for h in range(PER_GROUP):
                write(n, h, q[n * 128 : n * 128 + 128, h * 128 : h * 128 + 128])

    def write_send(n, h, value):
        q_send[n, h * 128 : h * 128 + 128, :] = value

    def write_own(n, h, value):
        q_all[core * 2 + n, h * 128 : h * 128 + 128, :] = value

    q_copy = remote(q_send, q_all.at[pl.ds(core * 2, 2)], sib_ssem.at[2], sib_rsem.at[2], sibling)

    def block_of(i, j):
        return pattern_t[j, core, chip * 4 + i]

    def score(i, pairs):
        q = q_all[i]
        best = None if pairs[0] == 0 else top[...]
        for p in pairs:
            keys = jnp.concatenate([key_table[block_of(i, 2 * p)], key_table[block_of(i, 2 * p + 1)]], axis=0)
            s = dot_nt(q, keys) * COEF
            left, right = s[:, 0:128] + bias[i, 2 * p], s[:, 128:256] + bias[i, 2 * p + 1]
            if p == 0:
                left = jnp.where(tri4, left, NEG)
            scores[p, :, 0:128] = left
            scores[p, :, 128:256] = right
            both = jnp.maximum(left, right)
            best = both if best is None else jnp.maximum(best, both)
        if pairs[-1] == PAIRS - 1:
            best = jnp.broadcast_to(jnp.max(best, axis=-1, keepdims=True), (512, 128))
        top[...] = best

    def weigh(i, pairs):
        total = None if pairs[0] == 0 else norms[i]
        for p in pairs:
            left = jnp.exp2(scores[p, :, 0:128] - top[...])
            right = jnp.exp2(scores[p, :, 128:256] - top[...])
            probs[i, :, p * 256 : p * 256 + 128] = left.astype(BF16)
            probs[i, :, p * 256 + 128 : p * 256 + 256] = right.astype(BF16)
            total = left + right if total is None else total + (left + right)
        if pairs[-1] == PAIRS - 1:
            total = jnp.broadcast_to(1.0 / jnp.sum(total, axis=-1, keepdims=True), (512, 128))
        norms[i] = total

    thirds = [range(0, 3), range(3, 6), range(6, 9)]
    work = [(f, i, pairs) for i in range(4) for f in (score, weigh) for pairs in thirds]
    work.reverse()

    def find_repeats(i, carry):
        entries = [pattern_t[j, core, chip * 4 + i] for j in range(SEL)]
        for j in range(SEL):
            value = jnp.float32(0.0)
            for e in range(j):
                value = jnp.where(entries[e] == entries[j], jnp.float32(NEG), value)
            bias[i, j] = value
        return carry


    waits = 0
    for copy, needs, starts in order:
        if needs is not None:
            if needs not in landed and waits == 0:
                put_queries(1, write_send)
                q_copy.start()
                waits = 1
            elif needs not in landed and waits == 1 and needs[0] != "sib":
                put_queries(0, write_own)
                lax.fori_loop(0, 4, find_repeats, 0)
                waits = 2
            land(needs)
            missing.discard(needs)
        if starts:
            launch(copy)
        if not missing and work:
            if len(work) == 24:
                q_copy.wait()
            part, i, pairs = work.pop()
            part(i, pairs)
    while work:
        part, i, pairs = work.pop()
        part(i, pairs)

    def attend(part, n):
        i = (1 - core if part == 0 else core) * 2 + n
        values = jnp.concatenate([value_table[block_of(i, j)] for j in range(SEL)], axis=0)
        out = dot(probs[i], values)
        rows = pl.ds(pl.multiple_of(n * 128, 128), 128)
        for h in range(PER_GROUP):
            value = (out[h * 128 : h * 128 + 128] * norms[i, h * 128 : h * 128 + 128, :]).astype(BF16)
            if part == 0:
                o_send[rows, h * 128 : h * 128 + 128] = value
            else:
                o_all[core, rows, h * 128 : h * 128 + 128] = value

    @pl.loop(0, 2)
    def _(n):
        attend(0, n)

    o_copy = remote(o_send, o_all.at[core], sib_ssem.at[3], sib_rsem.at[3], sibling)
    o_copy.start()

    @pl.loop(0, 2)
    def _(n):
        attend(1, n)

    for copy in [*st_copies, *tot_copies, *pre_copies, *sib_copies, *started.values()]:
        copy.wait_send()
    o_copy.wait()
    o_ref[:, 0:512] = o_all[0]
    o_ref[:, 512:1024] = o_all[1]


def local(hidden_in, lin_query, lin_key, lin_value, lin_gain, lin_out_weight, soft_gain, soft_wq, soft_wk, soft_wv, pattern):
    dma = pltpu.SemaphoreType.DMA
    vmem, anywhere = pl.BlockSpec(memory_space=pltpu.VMEM), pl.BlockSpec(memory_space=pl.ANY)
    scratch = [
        pltpu.VMEM((TOK, D), BF16),
        pltpu.VMEM((TOK, 1024), BF16),
        pltpu.VMEM((TOK, 256), BF16),
        pltpu.VMEM((TOK, 256), BF16),
        pltpu.VMEM((1024, D), BF16),
        pltpu.VMEM((2, D, 512), BF16),
        pltpu.VMEM((2, D, 256), BF16),
        pltpu.VMEM((2, NZ, 16, 128), BF16),
        pltpu.VMEM((2 * NZ, 16, 128), BF16),
        pltpu.VMEM((16, 128), F32),
        pltpu.VMEM((NX - 1, 16, 128), F32),
        pltpu.VMEM((2 * NZ, 16, 128), BF16),
        pltpu.VMEM((2, NZ, 16, 128), BF16),
        pltpu.VMEM((2, 128, 128), BF16),
        pltpu.VMEM((2, 2, 512, 128), BF16),
        pltpu.VMEM((TOK, 1024), BF16),
        pltpu.VMEM((TOK, D), BF16),
        pltpu.VMEM((TOK, D), BF16),
        pltpu.VMEM((2, TOK, 128), BF16),
        pltpu.VMEM((2, 512, 128), BF16),
        pltpu.VMEM((4, 512, 128), BF16),
        pltpu.VMEM((NX * NZ * CHIP_TOK // BLOCK, BLOCK, 128), BF16),
        pltpu.VMEM((NX * NZ * CHIP_TOK // BLOCK, BLOCK, 128), BF16),
        pltpu.VMEM((PAIRS, 512, 256), F32),
        pltpu.VMEM((4, 512, SEL * BLOCK), BF16),
        pltpu.VMEM((512, 128), F32),
        pltpu.VMEM((4, 512, 128), F32),
        pltpu.SMEM((4, SEL), F32),
        pltpu.VMEM((TOK, 512), BF16),
        pltpu.VMEM((2, TOK, 512), BF16),
        pltpu.SMEM((SEL, KV_HEADS, 128), jnp.int32),
        pltpu.VMEM((1, 1024), F32),
        pltpu.VMEM((1, D), F32),
        dma((14,)),
        dma((2 * NZ - 1,)), dma((2 * NZ - 1,)),
        dma((NX - 1,)), dma((NX - 1,)),
        dma((2 * NZ - 1,)), dma((2 * NZ - 1,)),
        dma((4,)), dma((4,)),
        dma((2, NX - 1)), dma((2, NX - 1)),
        dma((2, 2, 4, NX)), dma((2, 2, 4, NX)),
        dma((2, 2, 4)), dma((2, 2, 4)),
        dma((2, NZ, 3)), dma((2, NZ, 3)),
    ]
    return pl.pallas_call(
        kernel,
        name="mixer_and_attention",
        out_shape=jax.ShapeDtypeStruct((TOK, 1024), BF16),
        in_specs=[anywhere] * 11,
        out_specs=vmem,
        scratch_shapes=scratch,
        compiler_params=pltpu.CompilerParams(collective_id=0, has_side_effects=True, vmem_limit_bytes=56 << 20),
    )(
        pattern.transpose(2, 0, 1), lin_gain.reshape(1, 1024), soft_gain.reshape(1, D),
        hidden_in, lin_query, lin_key, lin_value, lin_out_weight, soft_wq, soft_wk, soft_wv,
    )


def solution(mesh):
    whole, split = P(), P(("dp", "seq"), None)
    in_specs = (split, split, split, split) + (whole,) * 7
    return jax.shard_map(local, mesh=mesh, in_specs=in_specs, out_specs=split, check_vma=False)
```

```python
import heapq
import math

import jax
import jax.numpy as jnp
from jax import lax
from jax.experimental import pallas as pl
from jax.experimental.pallas import tpu as pltpu
from jax.sharding import PartitionSpec as P

HEAD_DIM = 128
HEADS = 8
KV_HEADS = 2
PER_GROUP = HEADS // KV_HEADS
BLOCK = 128
SEL = 18
TOK = 256
D = 2048
NX, NZ = 4, 8
CHIP_TOK = 2 * TOK
PAIRS = SEL // 2
EPSILON = 1e-06
NEG = -1e30
COEF = HEAD_DIM ** (-0.5) * math.log2(math.e)
F32, BF16 = jnp.float32, jnp.bfloat16
MESH = pl.DeviceIdType.MESH

ROWS_A = 208
ROWS_B = CHIP_TOK - ROWS_A
FAR_FIRST = sorted(range(1, 2 * NZ), key=lambda i: -min(i, 2 * NZ - i))
ORDER = [(0, 0), (0, 1), (1, 1), (0, 2), (1, 2), (0, 3), (1, 3), (0, 4)]
STEPS = (4, 3)
LINK, LATENCY_US, SIBLING_US = 95000.0, 5.0, 3.0


def plan():
    ready, free, events, arrived, order = {"x": [], "z": []}, {"x": 0.0, "z": 0.0}, [], {}, []

    def add(copy, needs):
        kind, tensor = copy[:2]
        rank = (tensor, ("a1", "b1", "b2", "a2").index(kind), copy[3:] + copy[2:3] if kind in ("b1", "a2") else copy[2:])
        heapq.heappush(ready["x" if kind in ("a1", "b2") else "z"], (rank, copy, needs))

    def react(copy):
        kind, tensor, rest = copy[0], copy[1], copy[2:]
        if kind == "sib":
            for i in range(2):
                add(("b1", tensor, i, 1), copy)
                add(("b2", tensor, 0, i), copy)
        elif kind == "a1":
            add(("a2", tensor, 0, 1, rest[0]), copy)
            add(("a2", tensor, 1, 1, rest[0]), copy)
        elif kind == "b1":
            direction, step = rest
            if step < STEPS[direction]:
                add(("b1", tensor, direction, step + 1), copy)
            add(("b2", tensor, ORDER.index(rest), 0), copy)
            add(("b2", tensor, ORDER.index(rest), 1), copy)
        elif kind == "b2":
            if rest[1] == rest[0] % 2:
                add(("b2", tensor, rest[0], 2), copy)
        elif rest[1] < STEPS[rest[0]]:
            add(("a2", tensor, rest[0], rest[1] + 1, rest[2]), copy)

    for tensor in range(2):
        for i in (1, 3, 2):
            add(("a1", tensor, i), None)
        for i in range(2):
            add(("a2", tensor, i, 1, 0), None)
        heapq.heappush(events, (SIBLING_US + 0.5 * tensor, tensor, ("sib", tensor)))
    now, count = 0.0, 2
    while True:
        for link in "xz":
            if free[link] <= now and ready[link]:
                _, copy, needs = heapq.heappop(ready[link])
                order.append((now, copy, needs, True))
                rows = (ROWS_A if copy[0] in ("a1", "a2") else ROWS_B) * (2 if copy[0] == "a1" and copy[2] == 2 else 1)
                free[link] = now + rows * 256 / LINK
                arrived[copy] = free[link] + LATENCY_US
                order.append((arrived[copy], copy, copy, False))
                for event in ((arrived[copy], count, copy), (free[link], count + 1, None)):
                    heapq.heappush(events, event)
                count += 2
        if not events:
            return [step[1:] for step in sorted(order, key=lambda step: step[0])]
        now, _, copy = heapq.heappop(events)
        if copy:
            react(copy)


def dot(a, b):
    return jnp.dot(a, b, preferred_element_type=F32)


def dot_nt(a, b):
    return lax.dot_general(a, b, (((1,), (1,)), ((), ())), preferred_element_type=F32)


def dot_tn(a, b):
    return lax.dot_general(a, b, (((0,), (0,)), ((), ())), preferred_element_type=F32)


def kernel(
    pattern_hbm, lin_gain_hbm, soft_gain_hbm, hidden_hbm, lq_hbm, lk_hbm, lv_hbm, wo_hbm, wq_hbm, wk_hbm, wv_hbm,
    o_ref,
    hidden, lq, lk, lv, wo, wq, wkv, st_send, st_recv, tot_send, tot_recv, pre_send, pre_recv,
    block0, lin_scores, normed, resid, layer_in, kv_send, q_send, q_all, key_table, value_table, scores, probs, top, norms, bias,
    o_send, o_all,
    pattern_t, lin_gain, soft_gain,
    load_sem, st_ssem, st_rsem, tot_ssem, tot_rsem, pre_ssem, pre_rsem, sib_ssem, sib_rsem,
    a1_ssem, a1_rsem, a2_ssem, a2_rsem, b1_ssem, b1_rsem, b2_ssem, b2_rsem,
):
    me = lax.axis_index("seq")
    core = lax.rem(me, 2)
    chip = me // 2
    z = lax.rem(chip, NZ)
    x = chip // NZ
    sign = 1 - 2 * core
    row_pos = z * 2 + core

    def dev(cx, cz, cc):
        return {"seq": (lax.rem(cx + 2 * NX, NX) * NZ + lax.rem(cz + 2 * NZ, NZ)) * 2 + cc}

    sibling = dev(x, z, 1 - core)

    def remote(src, dst, ssem, rsem, device):
        return pltpu.make_async_remote_copy(
            src_ref=src, dst_ref=dst, send_sem=ssem, recv_sem=rsem, device_id=device, device_id_type=MESH
        )

    own_q = pl.ds(pl.multiple_of(core * 512, 512), 512)
    sib_q = pl.ds(pl.multiple_of((1 - core) * 512, 512), 512)
    own_h = pl.ds(pl.multiple_of(core * 128, 128), 128)
    sib_h = pl.ds(pl.multiple_of((1 - core) * 128, 128), 128)
    loads = [
        (lk_hbm, lk),
        (lv_hbm, lv),
        (lq_hbm, lq),
        (wo_hbm, wo),
        (hidden_hbm, hidden),
        (wk_hbm.at[:, own_h], wkv.at[0, :, 0:128]),
        (wv_hbm.at[:, own_h], wkv.at[0, :, 128:256]),
        (wk_hbm.at[:, sib_h], wkv.at[1, :, 0:128]),
        (wv_hbm.at[:, sib_h], wkv.at[1, :, 128:256]),
        (wq_hbm.at[:, own_q], wq.at[0]),
        (wq_hbm.at[:, sib_q], wq.at[1]),
        (lin_gain_hbm, lin_gain),
        (soft_gain_hbm, soft_gain),
        (pattern_hbm, pattern_t),
    ]
    loads = [pltpu.make_async_copy(src, dst, load_sem.at[i]) for i, (src, dst) in enumerate(loads)]
    for copy in loads[:3]:
        copy.start()

    barrier = pltpu.get_barrier_semaphore()
    for i in FAR_FIRST:
        pos = lax.rem(row_pos + i, 2 * NZ)
        pl.semaphore_signal(barrier, inc=1, device_id={"seq": x * 2 * NZ + pos}, device_id_type=MESH)
    for i in range(1, NX):
        pl.semaphore_signal(barrier, inc=1, device_id=dev(x + i, z, core), device_id_type=MESH)

    loads[0].wait()
    loads[1].wait()

    for g in range(KV_HEADS):
        cols = slice(g * 128, g * 128 + 128)
        first = dot_tn(lk[0:128, cols], lv[0:128, cols])
        second = dot_tn(lk[128:256, cols], lv[128:256, cols])
        block0[g] = first.astype(BF16)
        st_send[g] = (first + second).astype(BF16).reshape(NZ, 16, 128)

    pl.semaphore_wait(barrier, 2 * NZ - 1 + NX - 1)

    st_copies = []
    for i in FAR_FIRST:
        pos = lax.rem(row_pos + i, 2 * NZ)
        copy = remote(
            st_send.at[lax.rem(pos, 2), pos // 2], st_recv.at[row_pos], st_ssem.at[i - 1], st_rsem.at[i - 1],
            {"seq": x * 2 * NZ + pos},
        )
        copy.start()
        st_copies.append(copy)
    for copy in loads[3:]:
        copy.start()
    st_recv[row_pos] = st_send[core, z]

    loads[2].wait()
    tri = lax.broadcasted_iota(jnp.int32, (128, 128), 0) >= lax.broadcasted_iota(jnp.int32, (128, 128), 1)
    tri4 = jnp.concatenate([tri] * PER_GROUP, axis=0)

    def stacked(n, g):
        return jnp.concatenate(
            [lq[n * 128 : n * 128 + 128, (g * PER_GROUP + h) * 128 : (g * PER_GROUP + h) * 128 + 128] for h in range(PER_GROUP)],
            axis=0,
        )

    for n in range(2):
        for g in range(KV_HEADS):
            keys = lk[n * 128 : n * 128 + 128, g * 128 : g * 128 + 128]
            lin_scores[n, g] = jnp.where(tri4, dot_nt(stacked(n, g), keys), 0.0).astype(BF16)

    for copy in st_copies:
        copy.wait_recv()
    total = st_recv[0].astype(F32)
    for i in range(1, 2 * NZ):
        total = total + st_recv[i].astype(F32)
    tot_send[...] = total
    tot_copies = []
    for i in range(1, NX):
        copy = remote(tot_send, tot_recv.at[i - 1], tot_ssem.at[i - 1], tot_rsem.at[i - 1], dev(x + i, z, core))
        copy.start()
        tot_copies.append(copy)
    for copy in tot_copies:
        copy.wait_recv()
    running = jnp.zeros((16, 128), F32)
    for i in range(1, NX):
        running = running + jnp.where(x - i >= 0, tot_recv[i - 1], 0.0)
    for i in range(2 * NZ):
        pre_send[i] = running.astype(BF16)
        running = running + st_recv[i].astype(F32)
    pre_copies = []
    for i in FAR_FIRST:
        pos = lax.rem(row_pos + i, 2 * NZ)
        copy = remote(
            pre_send.at[pos], pre_recv.at[core, z], pre_ssem.at[i - 1], pre_rsem.at[i - 1], {"seq": x * 2 * NZ + pos}
        )
        copy.start()
        pre_copies.append(copy)
    pre_recv[core, z] = pre_send[row_pos]
    for copy in pre_copies:
        copy.wait_recv()

    loads[11].wait()
    loads[12].wait()
    loads[13].wait()
    for n in range(2):
        for g in range(KV_HEADS):
            state = pre_recv[g].reshape(128, 128)
            values = lv[n * 128 : n * 128 + 128, g * 128 : g * 128 + 128]
            if n == 0:
                mix = dot(
                    jnp.concatenate([stacked(n, g), lin_scores[n, g]], axis=1), jnp.concatenate([state, values], axis=0)
                )
            else:
                qs = stacked(n, g)
                mix = dot(
                    jnp.concatenate([qs, qs, lin_scores[n, g]], axis=1),
                    jnp.concatenate([state, block0[g], values], axis=0),
                )
            mix = mix * lax.rsqrt(jnp.mean(mix * mix, axis=-1, keepdims=True) + EPSILON)
            for h in range(PER_GROUP):
                cols = slice((g * PER_GROUP + h) * 128, (g * PER_GROUP + h) * 128 + 128)
                normed[n * 128 : n * 128 + 128, cols] = (mix[h * 128 : h * 128 + 128] * lin_gain[:, cols]).astype(BF16)

    loads[3].wait()
    loads[4].wait()
    squares = jnp.zeros((TOK, 128), F32)
    for t in range(4):
        cols = slice(t * 512, t * 512 + 512)
        res = (hidden[:, cols].astype(F32) + dot(normed[...], wo[:, cols])).astype(BF16)
        resid[:, cols] = res
        wide = res.astype(F32)
        wide = wide * wide
        for s in range(4):
            squares = squares + wide[:, s * 128 : s * 128 + 128]
    factor = lax.rsqrt(jnp.sum(squares, axis=-1, keepdims=True) * (1.0 / D) + EPSILON)
    for t in range(4):
        cols = slice(t * 512, t * 512 + 512)
        layer_in[:, cols] = (resid[:, cols].astype(F32) * factor * soft_gain[:, cols]).astype(BF16)

    for i in range(5, 9):
        loads[i].wait()
    tables = [t.reshape(NX * NZ * CHIP_TOK, 128) for t in (key_table, value_table)]
    my_rows = pl.ds(pl.multiple_of(me * TOK, TOK), TOK)
    sib_copies = []
    both = dot(layer_in[...], wkv[1]).astype(BF16)
    for tensor in range(2):
        kv_send[tensor] = both[:, tensor * 128 : tensor * 128 + 128]
        copy = remote(kv_send.at[tensor], tables[tensor].at[my_rows], sib_ssem.at[tensor], sib_rsem.at[tensor], sibling)
        copy.start()
        sib_copies.append(copy)
    both = dot(layer_in[...], wkv[0]).astype(BF16)
    for tensor in range(2):
        tables[tensor][my_rows] = both[:, tensor * 128 : tensor * 128 + 128]

    started, landed = {}, set()
    sems = {"a1": (a1_ssem, a1_rsem), "a2": (a2_ssem, a2_rsem), "b1": (b1_ssem, b1_rsem), "b2": (b2_ssem, b2_rsem)}

    def launch(copy):
        kind, tensor, rest = copy[0], copy[1], copy[2:]

        def hop(direction, distance):
            return (-sign if direction == 0 else sign) * distance

        sx, sz = x, z
        if kind == "a1":
            index, to = (rest[0] - 1,), dev(x + rest[0], z, core)
        elif kind == "b1":
            sz, index = z + hop(rest[0], rest[1] - 1), (rest[0], rest[1] - 1)
            to = dev(x, z - hop(rest[0], 1), core)
        elif kind == "a2":
            sx, sz, index = x - rest[2], z + hop(rest[0], rest[1] - 1), (rest[0], rest[1] - 1, rest[2])
            to = dev(x, z - hop(rest[0], 1), core)
        else:
            r, j = rest
            sz, index = z + hop(*ORDER[r]), (r, j)
            along = (sign, -sign)[j if j < 2 else r % 2]
            if j == 2:
                sx = x - along
            to = dev(x + along, z, core)
        if kind in ("a1", "a2"):
            first, count = core * ROWS_B, ROWS_A
        else:
            first, count = (1 - core) * ROWS_A, ROWS_B
        src = lax.rem(sx + 2 * NX, NX) * NZ + lax.rem(sz + 2 * NZ, NZ)
        part = tables[tensor].at[pl.ds(pl.multiple_of(src * CHIP_TOK + first, 16), count)]
        ssem, rsem = sems[kind]
        started[copy] = remote(part, part, ssem.at[(tensor, *index)], rsem.at[(tensor, *index)], to)
        started[copy].start()

    def land(copy):
        if copy not in landed:
            landed.add(copy)
            (sib_copies[copy[1]] if copy[0] == "sib" else started[copy]).wait_recv()

    order = plan()
    missing = {copy for copy, _, _ in order if copy[1] == 0}
    loads[9].wait()
    loads[10].wait()

    def put_queries(part, write):
        q = dot(layer_in[...], wq[part]).astype(BF16)
        for n in range(2):
            for h in range(PER_GROUP):
                write(n, h, q[n * 128 : n * 128 + 128, h * 128 : h * 128 + 128])

    def write_send(n, h, value):
        q_send[n, h * 128 : h * 128 + 128, :] = value

    def write_own(n, h, value):
        q_all[core * 2 + n, h * 128 : h * 128 + 128, :] = value

    q_copy = remote(q_send, q_all.at[pl.ds(core * 2, 2)], sib_ssem.at[2], sib_rsem.at[2], sibling)

    def block_of(i, j):
        return pattern_t[j, core, chip * 4 + i]

    def score(i, pairs):
        q = q_all[i]
        best = None if pairs[0] == 0 else top[...]
        for p in pairs:
            keys = jnp.concatenate([key_table[block_of(i, 2 * p)], key_table[block_of(i, 2 * p + 1)]], axis=0)
            s = dot_nt(q, keys) * COEF
            left, right = s[:, 0:128] + bias[i, 2 * p], s[:, 128:256] + bias[i, 2 * p + 1]
            if p == 0:
                left = jnp.where(tri4, left, NEG)
            scores[p, :, 0:128] = left
            scores[p, :, 128:256] = right
            both = jnp.maximum(left, right)
            best = both if best is None else jnp.maximum(best, both)
        if pairs[-1] == PAIRS - 1:
            best = jnp.broadcast_to(jnp.max(best, axis=-1, keepdims=True), (512, 128))
        top[...] = best

    def weigh(i, pairs):
        total = None if pairs[0] == 0 else norms[i]
        for p in pairs:
            left = jnp.exp2(scores[p, :, 0:128] - top[...])
            right = jnp.exp2(scores[p, :, 128:256] - top[...])
            probs[i, :, p * 256 : p * 256 + 128] = left.astype(BF16)
            probs[i, :, p * 256 + 128 : p * 256 + 256] = right.astype(BF16)
            total = left + right if total is None else total + (left + right)
        if pairs[-1] == PAIRS - 1:
            total = jnp.broadcast_to(1.0 / jnp.sum(total, axis=-1, keepdims=True), (512, 128))
        norms[i] = total

    thirds = [range(0, 3), range(3, 6), range(6, 9)]
    work = [(f, i, pairs) for i in range(4) for f in (score, weigh) for pairs in thirds]
    work.reverse()

    def find_repeats(i, carry):
        entries = [pattern_t[j, core, chip * 4 + i] for j in range(SEL)]
        for j in range(SEL):
            value = jnp.float32(0.0)
            for e in range(j):
                value = jnp.where(entries[e] == entries[j], jnp.float32(NEG), value)
            bias[i, j] = value
        return carry


    waits = 0
    for copy, needs, starts in order:
        if needs is not None:
            if needs not in landed and waits == 0:
                put_queries(1, write_send)
                q_copy.start()
                waits = 1
            elif needs not in landed and waits == 1 and needs[0] != "sib":
                put_queries(0, write_own)
                lax.fori_loop(0, 4, find_repeats, 0)
                waits = 2
            land(needs)
            missing.discard(needs)
        if starts:
            launch(copy)
        if not missing and work:
            if len(work) == 24:
                q_copy.wait()
            part, i, pairs = work.pop()
            part(i, pairs)
    while work:
        part, i, pairs = work.pop()
        part(i, pairs)

    def attend(part, n):
        i = (1 - core if part == 0 else core) * 2 + n
        values = jnp.concatenate([value_table[block_of(i, j)] for j in range(SEL)], axis=0)
        out = dot(probs[i], values)
        rows = pl.ds(n * 128 if part == 0 else pl.multiple_of(n * 128, 128), 128)
        for h in range(PER_GROUP):
            value = (out[h * 128 : h * 128 + 128] * norms[i, h * 128 : h * 128 + 128, :]).astype(BF16)
            if part == 0:
                o_send[rows, h * 128 : h * 128 + 128] = value
            else:
                o_all[core, rows, h * 128 : h * 128 + 128] = value

    o_copies = []
    for n in range(2):
        attend(0, n)
        half = pl.ds(n * 128, 128)
        o_copies.append(remote(o_send.at[half], o_all.at[core, half], sib_ssem.at[3 + n], sib_rsem.at[3 + n], sibling))
        o_copies[n].start()

    @pl.loop(0, 2)
    def _(n):
        attend(1, n)

    for copy in [*st_copies, *tot_copies, *pre_copies, *sib_copies, *started.values()]:
        copy.wait_send()
    for copy in o_copies:
        copy.wait()
    o_ref[:, 0:512] = o_all[0]
    o_ref[:, 512:1024] = o_all[1]


def local(hidden_in, lin_query, lin_key, lin_value, lin_gain, lin_out_weight, soft_gain, soft_wq, soft_wk, soft_wv, pattern):
    dma = pltpu.SemaphoreType.DMA
    vmem, anywhere = pl.BlockSpec(memory_space=pltpu.VMEM), pl.BlockSpec(memory_space=pl.ANY)
    scratch = [
        pltpu.VMEM((TOK, D), BF16),
        pltpu.VMEM((TOK, 1024), BF16),
        pltpu.VMEM((TOK, 256), BF16),
        pltpu.VMEM((TOK, 256), BF16),
        pltpu.VMEM((1024, D), BF16),
        pltpu.VMEM((2, D, 512), BF16),
        pltpu.VMEM((2, D, 256), BF16),
        pltpu.VMEM((2, NZ, 16, 128), BF16),
        pltpu.VMEM((2 * NZ, 16, 128), BF16),
        pltpu.VMEM((16, 128), F32),
        pltpu.VMEM((NX - 1, 16, 128), F32),
        pltpu.VMEM((2 * NZ, 16, 128), BF16),
        pltpu.VMEM((2, NZ, 16, 128), BF16),
        pltpu.VMEM((2, 128, 128), BF16),
        pltpu.VMEM((2, 2, 512, 128), BF16),
        pltpu.VMEM((TOK, 1024), BF16),
        pltpu.VMEM((TOK, D), BF16),
        pltpu.VMEM((TOK, D), BF16),
        pltpu.VMEM((2, TOK, 128), BF16),
        pltpu.VMEM((2, 512, 128), BF16),
        pltpu.VMEM((4, 512, 128), BF16),
        pltpu.VMEM((NX * NZ * CHIP_TOK // BLOCK, BLOCK, 128), BF16),
        pltpu.VMEM((NX * NZ * CHIP_TOK // BLOCK, BLOCK, 128), BF16),
        pltpu.VMEM((PAIRS, 512, 256), F32),
        pltpu.VMEM((4, 512, SEL * BLOCK), BF16),
        pltpu.VMEM((512, 128), F32),
        pltpu.VMEM((4, 512, 128), F32),
        pltpu.SMEM((4, SEL), F32),
        pltpu.VMEM((TOK, 512), BF16),
        pltpu.VMEM((2, TOK, 512), BF16),
        pltpu.SMEM((SEL, KV_HEADS, 128), jnp.int32),
        pltpu.VMEM((1, 1024), F32),
        pltpu.VMEM((1, D), F32),
        dma((14,)),
        dma((2 * NZ - 1,)), dma((2 * NZ - 1,)),
        dma((NX - 1,)), dma((NX - 1,)),
        dma((2 * NZ - 1,)), dma((2 * NZ - 1,)),
        dma((5,)), dma((5,)),
        dma((2, NX - 1)), dma((2, NX - 1)),
        dma((2, 2, 4, NX)), dma((2, 2, 4, NX)),
        dma((2, 2, 4)), dma((2, 2, 4)),
        dma((2, NZ, 3)), dma((2, NZ, 3)),
    ]
    return pl.pallas_call(
        kernel,
        name="mixer_and_attention",
        out_shape=jax.ShapeDtypeStruct((TOK, 1024), BF16),
        in_specs=[anywhere] * 11,
        out_specs=vmem,
        scratch_shapes=scratch,
        compiler_params=pltpu.CompilerParams(collective_id=0, has_side_effects=True, vmem_limit_bytes=56 << 20),
    )(
        pattern.transpose(2, 0, 1), lin_gain.reshape(1, 1024), soft_gain.reshape(1, D),
        hidden_in, lin_query, lin_key, lin_value, lin_out_weight, soft_wq, soft_wk, soft_wv,
    )


def solution(mesh):
    whole, split = P(), P(("dp", "seq"), None)
    in_specs = (split, split, split, split) + (whole,) * 7
    return jax.shard_map(local, mesh=mesh, in_specs=in_specs, out_specs=split, check_vma=False)
```
